512 devices in a mesh: gz: 4 (over x), gy: 16 (over z, y_hi), gx: 8 (over y_lo, core).
Axes of the slice: x: 4, y: 8 (y_hi: 2, y_lo: 4; y = y_hi * 4 + y_lo), z: 8, core: 2. Of those that a mesh axis runs over, the one named last changes fastest.
Arguments:
- volume: bfloat16 [32, 16, 128, 384], P('gz', 'gy', 'gx'), may hold values from -80 to 80
- cotangent: bfloat16 [32, 16, 128, 384], P('gz', 'gy', 'gx'), may hold values from -6 to 6
- w_project: bfloat16 [3, 384, 1152], P(None, 'gy', ('gz', 'gx')), may hold values from -0.3125 to 0.3125
- w_output: bfloat16 [3, 384, 384], P(None, 'gy', ('gz', 'gx')), may hold values from -0.3125 to 0.3125
Outputs:
- grad_volume: bfloat16 [32, 16, 128, 384], P('gz', 'gy', 'gx')
The draws below stay inside these ranges and needn't reach their ends.
All inputs are finite; a program needn't handle non-finite values.
Results may differ from the reference program's by a relative error of at most 0.015.
Values may be sent and summed in bfloat16 or wider, within the bound.
A program may use at most 64 MiB of HBM per device.

```python
import math
import jax
import jax.numpy as jnp
from jax import lax

D = 384
HEADS = 6
Z = 32
Y = 16
X = 128


def draw_volume(key, part):
    base_key, row_key, col_key = jax.random.split(jax.random.fold_in(key, 7), 3)
    rough_part = jnp.clip(jax.random.normal(base_key, (Z, Y, X, D), jnp.float32), -4.0, 4.0)
    row_scale = jnp.exp(jax.random.uniform(row_key, (Z, Y, X, 1), jnp.float32, 0.0, math.log(10.0)))
    col_scale = jnp.exp(jax.random.uniform(col_key, (1, 1, 1, D), jnp.float32, -math.log(2.0), math.log(2.0)))
    return (rough_part * row_scale * col_scale).astype(jnp.bfloat16)


def levels(own_key, extent, shards, low, top_value):
    level, own = 1.0, jax.random.fold_in(own_key, 6)
    for axis_at, parts in shards:
        heights = jnp.exp(jax.random.uniform(jax.random.fold_in(own, axis_at), (parts,), jnp.float32, low / len(shards), top_value / len(shards)))
        level = level * jnp.repeat(heights, extent[axis_at] // parts).reshape([-1 if axis == axis_at else 1 for axis in range(len(extent))])
    return level


def noise(key, dims, width, limit, cuts=(), held_as=jnp.bfloat16):
    loudness = levels(key, dims, cuts, -0.22, 0.18) if cuts else 1.0
    values = jax.random.normal(key, dims, jnp.float32) * width * loudness
    return jnp.minimum(jnp.maximum(values, -limit), limit).astype(held_as)


def setup_inputs(seed: int = 0) -> dict:
    streams_of = jax.random.split(jax.random.key(seed), 5)
    volume = draw_volume(jax.random.fold_in(streams_of[4], 71), 0)
    cotangent = noise(streams_of[1], (Z, Y, X, D), 1.0, 6.0, ((0, 4), (1, 16), (2, 8)))
    w_project = noise(streams_of[2], (3, D, 3 * D), D ** -0.5, 0.3125, ((1, 16), (2, 32)))
    w_output = noise(streams_of[3], (3, D, D), D ** -0.5, 0.3125, ((1, 16), (2, 32)))
    return dict(volume=volume, cotangent=cotangent, w_project=w_project, w_output=w_output)


def head_norm(vector):
    return (vector * lax.rsqrt(lax.optimization_barrier(jnp.mean(vector * vector, axis=-1, keepdims=True)) + 1e-06)).astype(jnp.bfloat16)

def sublayer(line_rows, w_inner, w_outer):
    feat_len = line_rows.shape[-1]
    head_size = feat_len // HEADS
    stream = line_rows.astype(jnp.float32)
    normed = (stream * lax.rsqrt(lax.optimization_barrier(jnp.mean(stream * stream, axis=-1, keepdims=True)) + 1e-06)).astype(jnp.bfloat16)
    packed = jnp.dot(normed, w_inner, preferred_element_type=jnp.float32)
    head_shape = line_rows.shape[:3] + (HEADS, head_size)
    queries = head_norm(packed[..., :feat_len].reshape(head_shape))
    key_part = head_norm(packed[..., feat_len:2 * feat_len].reshape(head_shape))
    value_part = packed[..., 2 * feat_len:].reshape(head_shape).astype(jnp.bfloat16)
    scores = jnp.einsum('plqhe,pkqhe->pqhlk', queries.astype(jnp.float32), key_part.astype(jnp.float32)) * head_size ** (-0.5)
    powers = jnp.exp(scores)
    attn_weights = (powers / lax.optimization_barrier(jnp.sum(powers, axis=-1, keepdims=True))).astype(jnp.bfloat16)
    mixed_out = jnp.einsum('pqhlk,pkqhe->plqhe', attn_weights.astype(jnp.float32), value_part.astype(jnp.float32))
    mixed_out = mixed_out.astype(jnp.bfloat16).reshape(line_rows.shape)
    update = jnp.dot(mixed_out, w_outer, preferred_element_type=jnp.float32)
    return (stream + update).astype(jnp.bfloat16)

def along_axis(field, direction, w_inner, w_outer):
    if direction == 'depth':

        def one_slice(piece):
            return sublayer(piece[None], w_inner, w_outer)[0]
        moved = jnp.moveaxis(field, 1, 0)
        return jnp.moveaxis(lax.map(jax.checkpoint(one_slice), moved), 0, 1)
    if direction == 'rows':

        def one_slice(piece):
            return sublayer(piece[None], w_inner, w_outer)[0]
        return lax.map(jax.checkpoint(one_slice), field)

    def one_slice(piece):
        return sublayer(piece[:, :, None, :], w_inner, w_outer)[:, :, 0, :]
    return lax.map(jax.checkpoint(one_slice), field)

def reference(volume, cotangent, w_project, w_output):

    def forward(field):
        field = along_axis(field, 'depth', w_project[0], w_output[0])
        field = along_axis(field, 'rows', w_project[1], w_output[1])
        return along_axis(field, 'columns', w_project[2], w_output[2])
    _, pullback = jax.vjp(forward, volume)
    return pullback(cotangent)[0]
```

```python
import functools

import jax
import jax.numpy as jnp
from jax import lax
from jax.experimental import pallas as pl
from jax.experimental.pallas import tpu as pltpu
from jax.sharding import PartitionSpec as P

MESH = pl.DeviceIdType.MESH
F32 = jnp.float32
BF16 = jnp.bfloat16
HEADS = 6
HEAD = 64
D = 384
EPS = 1e-06
TOK = 128
NZ, NY, NX = 4, 16, 8
NG = NZ * NX
QKV = 36
OUT = 12
CH = QKV + OUT
ROWS = 24


def dot(a, b, ca, cb):
    return lax.dot_general(a, b, (((ca,), (cb,)), ((), ())), preferred_element_type=F32)


def roll4(x):
    return pltpu.roll(x, 4, x.ndim - 2)


def low_half(shape):
    return lax.broadcasted_iota(jnp.int32, shape, len(shape) - 2) % 8 < 4


def swap_halves(u, v):
    low = low_half(u.shape)
    return jnp.where(low, u, roll4(v)), jnp.where(low, roll4(u), v)


def forward(stream, w_t, wo_t, mask, save):
    inv = lax.rsqrt(jnp.mean(stream * stream, axis=-1, keepdims=True) + EPS)
    normed = (stream * inv).astype(BF16)
    packed = dot(w_t, normed, 1, 1)
    heads = packed.reshape(3, HEADS, HEAD, TOK)
    inv_qk = lax.rsqrt(jnp.mean(heads[:2] * heads[:2], axis=2, keepdims=True) + EPS)
    qk = (heads[:2] * inv_qk).astype(BF16)
    val = heads[2].astype(BF16)
    mixed = []
    for h in range(HEADS):
        scores = dot(qk[1, h], qk[0, h], 0, 0) * (HEAD**-0.5)
        powers = jnp.exp(scores)
        if mask is not None:
            powers = jnp.where(mask, powers, 0.0)
        attn = (powers / jnp.sum(powers, axis=0, keepdims=True)).astype(BF16)
        save["attn"][h] = attn
        mixed.append(dot(val[h], attn, 1, 0).astype(BF16))
    mixed = jnp.concatenate(mixed, axis=0)
    save["inv"][...] = inv
    save["normed"][...] = normed
    save["inv_qk"][...] = inv_qk.reshape(2 * HEADS, 1, TOK)
    save["qkv"][: 2 * HEADS] = qk.reshape(2 * HEADS, HEAD, TOK)
    save["qkv"][2 * HEADS :] = val
    if wo_t is None:
        return None
    return stream + dot(wo_t, mixed, 1, 0).T


def backward(grad, w_t, wo_t, save):
    mixed_grad = dot(grad, wo_t, 1, 0).T.astype(BF16)
    packed_grad = [None] * (3 * HEADS)
    for h in range(HEADS):
        q, k, v = save["qkv"][h], save["qkv"][HEADS + h], save["qkv"][2 * HEADS + h]
        attn = save["attn"][h]
        attn32 = attn.astype(F32)
        d_mixed = mixed_grad[h * HEAD : (h + 1) * HEAD]
        d_attn = dot(v, d_mixed, 0, 0)
        d_v = dot(d_mixed, attn, 1, 1)
        d_scores = attn32 * (d_attn - jnp.sum(d_attn * attn32, axis=0, keepdims=True))
        d_scores = (d_scores * (HEAD**-0.5)).astype(BF16)
        d_q = dot(k, d_scores, 1, 0)
        d_k = dot(q, d_scores, 1, 1)
        for at, unit, d_unit in ((h, q, d_q), (HEADS + h, k, d_k)):
            unit32 = unit.astype(F32)
            proj = jnp.mean(d_unit * unit32, axis=0, keepdims=True)
            packed_grad[at] = (save["inv_qk"][at] * (d_unit - unit32 * proj)).astype(BF16)
        packed_grad[2 * HEADS + h] = d_v.astype(BF16)
    packed_grad = jnp.concatenate(packed_grad, axis=0)
    d_normed = dot(packed_grad, w_t, 0, 0)
    normed32 = save["normed"][...].astype(F32)
    proj = jnp.mean(d_normed * normed32, axis=-1, keepdims=True)
    return grad.astype(F32) + save["inv"][...] * (d_normed - normed32 * proj)


def line_mask(lines):
    row = lax.broadcasted_iota(jnp.int32, (TOK, TOK), 0)
    col = lax.broadcasted_iota(jnp.int32, (TOK, TOK), 1)
    return row % lines == col % lines


def split_home(block, out):
    x = block.astype(F32).reshape(4, 2, 2, 8, D)
    for half in range(2):
        low, high = swap_halves(x[:, 0, half], x[:, 1, half])
        out[2 * half] = low.reshape(32, D).astype(BF16)
        out[2 * half + 1] = high.reshape(32, D).astype(BF16)


def join_home(got, out):
    for half in range(2):
        u = got[2 * half].astype(F32).reshape(4, 8, D)
        v = got[2 * half + 1].astype(F32).reshape(4, 8, D)
        low, high = swap_halves(u, v)
        for m in range(4):
            out[2 * m, 8 * half : 8 * half + 8] = low[m].astype(BF16)
            out[2 * m + 1, 8 * half : 8 * half + 8] = high[m].astype(BF16)


def pack8(x, out):
    x = x.reshape(NY, 8, D)
    out[:, 0:16] = jnp.concatenate([x[:, :, 0:128], x[:, :, 128:256]], axis=1).astype(BF16)
    out[:, 16:32] = jnp.concatenate([x[:, :, 256:384], x[:, :, 256:384]], axis=1).astype(BF16)


def unpack8(got):
    x = got[...].astype(F32)
    return jnp.concatenate([x[:, 0:8], x[:, 8:16], x[:, 16:24]], axis=2).reshape(TOK, D)


def pack4(x, out):
    x = x.reshape(16, 8, D)
    first, second, third = x[:, :, 0:128], x[:, :, 128:256], x[:, :, 256:384]
    low, high = swap_halves(first, second)
    out[:, 0] = jnp.concatenate([low, third], axis=1).astype(BF16)
    out[:, 1] = jnp.concatenate([high, roll4(third)], axis=1).astype(BF16)


def unpack4(got):
    even, odd = got[:, 0].astype(F32), got[:, 1].astype(F32)
    first, second = swap_halves(even[:, 0:8], odd[:, 0:8])
    third = swap_halves(even[:, 8:16], odd[:, 8:16])[0]
    return jnp.concatenate([first, second, third], axis=2).reshape(TOK, D)


def own_chunk(w_ref, wo_ref, stage):
    rows = 3 * ROWS
    eye = (
        lax.broadcasted_iota(jnp.int32, (rows, 128), 0) == lax.broadcasted_iota(jnp.int32, (rows, 128), 1)
    ).astype(BF16)
    stage[0:QKV] = dot(w_ref[...], eye, 0, 0)
    stage[QKV:CH] = dot(wo_ref[...], eye, 0, 0)
    return stage[...].astype(BF16)


def join_features(parts, layer):
    lane = lax.broadcasted_iota(jnp.int32, (CH, 128), 1)
    tiles = []
    for t in range(3):
        tile = None
        for g in range(NY):
            start = ROWS * g - 128 * t
            if start + ROWS <= 0 or start >= 128:
                continue
            piece = pltpu.roll(parts[g], (start - ROWS * layer) % 128, 1)
            tile = piece if tile is None else jnp.where(lane >= start, piece, tile)
        tiles.append(tile)
    return jnp.concatenate(tiles, axis=1)


def slot_of(unit):
    return (unit % 2) * 16 + (unit // 8) * 4 + (unit % 8) // 2


def compact(gathered, layer, w_t, wo_t, stage):
    for unit in range(NG):
        chunk = gathered[layer, slot_of(unit)].astype(F32)
        stage[QKV * unit : QKV * (unit + 1)] = chunk[:QKV]
        stage[3 * D + OUT * unit : 3 * D + OUT * (unit + 1)] = chunk[QKV:]
    w_t[layer] = stage[: 3 * D].astype(BF16)
    wo_t[layer] = stage[3 * D :].astype(BF16)


def kernel(
    vol, cot, w_in, wo_in, out,
    h1s, h1r, h2s, h2r, h3s, h3r, g3s, g3r, g2s, g2r, g1s, g1r, cotr,
    wsend, wparts, gathered, w_t, wo_t, wstage, cstage,
    *rest,
):
    saves = []
    for i in range(3):
        a, b, c, d, e = rest[5 * i : 5 * i + 5]
        saves.append(dict(attn=a, inv=b, normed=c, inv_qk=d, qkv=e))
    a2a_send, a2a_recv, cot_send, cot_recv, w_sems, wy_send, wy_recv, wx_send, wx_recv, wc_send, wc_recv = rest[15:]
    gz, gy, gx = lax.axis_index("gz"), lax.axis_index("gy"), lax.axis_index("gx")
    core, ylo = gx % 2, gx // 2
    line = ((gz + NZ - 1) % NZ) * NX + gx
    column = gx * NZ + gz

    def line_owner(d):
        return (d // NX + 1) % NZ, d % NX

    def column_owner(s):
        return s % NZ, s // NZ

    def send(src, dst, ssem, rsem, to):
        pltpu.make_async_remote_copy(
            src_ref=src, dst_ref=dst, send_sem=ssem, recv_sem=rsem, device_id=to, device_id_type=MESH
        ).start()

    def drain(ref, sem):
        pltpu.make_async_copy(ref, ref, sem).wait()

    def each(count, body):
        lax.fori_loop(0, count, lambda k, c: (body(k), c)[1], 0)

    barrier = pltpu.get_barrier_semaphore()

    def greet(to):
        pl.semaphore_signal(barrier, inc=1, device_id=to, device_id_type=MESH)

    each(NY - 1, lambda k: greet((gz, (gy + 1 + k) % NY, gx)))

    def greet_line(k):
        s = (column + 1 + k) % NG
        z, x = column_owner(s)
        greet((z, gy, x))

    each(NG - 1, greet_line)
    each(NX, lambda k: greet((gy // 4, line // 2, k)))

    wsend[...] = own_chunk(w_in, wo_in, cstage)
    split_home(vol[...], h1s)
    pl.semaphore_wait(barrier, NY - 1 + NG - 1 + 8)

    each(
        NY - 1,
        lambda k: send(wsend, wparts.at[gy], w_sems.at[0], w_sems.at[1], (gz, (gy + 1 + k) % NY, gx)),
    )
    pltpu.make_async_copy(wsend, wparts.at[gy], w_sems.at[1]).start()

    def gz_exchange(src, dst, n):
        def body(k):
            to = (gz + 1 + k) % NZ
            send(src.at[to], dst.at[gz], a2a_send.at[n], a2a_recv.at[n], (to, gy, gx))

        each(NZ - 1, body)
        pltpu.make_async_copy(src.at[gz], dst.at[gz], a2a_recv.at[n]).start()

    def gy_exchange(src, dst, n):
        def body(k):
            to = (gy + 1 + k) % NY
            send(src.at[to], dst.at[gy], a2a_send.at[n], a2a_recv.at[n], (gz, to, gx))

        each(NY - 1, body)
        pltpu.make_async_copy(src.at[gy], dst.at[gy], a2a_recv.at[n]).start()

    gz_exchange(h1s, h1r, 0)

    def send_cot(k):
        z, x = line_owner(2 * gy + k % 2)
        send(cot.at[k], cotr.at[gx], cot_send, cot_recv, (z, 4 * gz + k // 2, x))

    each(8, send_cot)

    drain(wparts, w_sems.at[1])
    parts = wparts[...].astype(F32)
    own = gz * 4 + ylo
    for layer in range(3):
        gathered[layer, core * 16 + own] = join_features(parts, layer).astype(BF16)

        def send_y(k, layer=layer):
            to = (ylo + 1 + k) % 4
            block = gathered.at[layer, core * 16 + own]
            send(block, block, wy_send.at[layer], wy_recv.at[layer], (gz, gy, to * 2 + core))

        each(3, send_y)

    def run4(layer, c, z):
        return gathered.at[layer, pl.ds(c * 16 + z * 4, 4)]

    for layer in range(3):
        drain(gathered.at[layer, pl.ds(0, 3)], wy_recv.at[layer])
        mine = run4(layer, core, gz)

        def send_x(k, layer=layer, mine=mine):
            to = (gz + 1 + k) % NZ
            send(mine, mine, wx_send.at[layer], wx_recv.at[layer, gz], (to, gy, gx))

        each(3, send_x)
        send(mine, mine, wc_send.at[layer], wc_recv.at[layer], (gz, gy, gx + 1 - 2 * core))

    def finish_weights(layer):
        def forward_x(k):
            z = (gz + 1 + k) % NZ
            block = run4(layer, core, z)
            drain(block, wx_recv.at[layer, z])
            send(block, block, wc_send.at[layer], wc_recv.at[layer], (gz, gy, gx + 1 - 2 * core))

        each(3, forward_x)
        drain(gathered.at[layer, pl.ds(0, 16)], wc_recv.at[layer])
        compact(gathered, layer, w_t, wo_t, wstage)

    finish_weights(0)
    drain(h1r, a2a_recv.at[0])
    depth_mask = line_mask(4)
    x = h1r[...].reshape(TOK, D).astype(F32)
    x = forward(x, w_t[0], wo_t[0], depth_mask, saves[0])
    pack8(x, h2s)
    gy_exchange(h2s, h2r, 1)

    finish_weights(1)
    drain(h2r, a2a_recv.at[1])
    row_mask = line_mask(8)
    x = forward(unpack8(h2r), w_t[1], wo_t[1], row_mask, saves[1])
    pack4(x, h3s)

    def line_exchange(src, dst, n):
        def body(k):
            d = (line + 1 + k) % NG
            z, x = line_owner(d)
            send(src.at[d // 2, d % 2], dst.at[column // 2, column % 2], a2a_send.at[n], a2a_recv.at[n], (z, gy, x))

        each(NG - 1, body)
        pltpu.make_async_copy(
            src.at[line // 2, line % 2], dst.at[column // 2, column % 2], a2a_recv.at[n]
        ).start()

    def column_exchange(src, dst, n):
        def body(k):
            s = (column + 1 + k) % NG
            z, x = column_owner(s)
            send(src.at[s // 2, s % 2], dst.at[line // 2, line % 2], a2a_send.at[n], a2a_recv.at[n], (z, gy, x))

        each(NG - 1, body)
        pltpu.make_async_copy(
            src.at[column // 2, column % 2], dst.at[line // 2, line % 2], a2a_recv.at[n]
        ).start()

    line_exchange(h3s, h3r, 2)

    finish_weights(2)
    drain(cotr, cot_recv)
    drain(h3r, a2a_recv.at[2])
    forward(unpack4(h3r), w_t[2], None, None, saves[2])
    g = backward(cotr[...].reshape(TOK, D), w_t[2], wo_t[2], saves[2])
    pack4(g, g3s)
    column_exchange(g3s, g3r, 3)

    drain(g3r, a2a_recv.at[3])
    g = backward(unpack4(g3r).astype(BF16), w_t[1], wo_t[1], saves[1])
    pack8(g, g2s)
    gy_exchange(g2s, g2r, 4)

    drain(g2r, a2a_recv.at[4])
    g = backward(unpack8(g2r).astype(BF16), w_t[0], wo_t[0], saves[0])
    g1s[...] = g.astype(BF16).reshape(NZ, 32, D)
    gz_exchange(g1s, g1r, 5)

    drain(wparts.at[pl.ds(0, NY - 1)], w_sems.at[0])
    drain(h1r.at[pl.ds(0, NZ - 1)], a2a_send.at[0])
    drain(cotr, cot_send)
    for layer in range(3):
        drain(gathered.at[layer, pl.ds(0, 3)], wy_send.at[layer])
        drain(gathered.at[layer, pl.ds(0, 12)], wx_send.at[layer])
        drain(gathered.at[layer, pl.ds(0, 16)], wc_send.at[layer])
    for n, ref in ((1, h2r), (4, g2r)):
        drain(ref.at[pl.ds(0, NY - 1)], a2a_send.at[n])
    for n, ref in ((2, h3r), (3, g3r)):
        drain(ref.at[pl.ds(0, 15)], a2a_send.at[n])
        drain(ref.at[15, pl.ds(0, 1)], a2a_send.at[n])
    drain(g1r.at[pl.ds(0, NZ - 1)], a2a_send.at[5])

    drain(g1r, a2a_recv.at[5])
    join_home(g1r, out)


def local(volume, cotangent, w_project, w_output):
    vmem = pltpu.VMEM
    save = [
        vmem((HEADS, TOK, TOK), BF16),
        vmem((TOK, 1), F32),
        vmem((TOK, D), BF16),
        vmem((2 * HEADS, 1, TOK), F32),
        vmem((3 * HEADS, HEAD, TOK), BF16),
    ]
    dma = pltpu.SemaphoreType.DMA
    scratch = [
        *[vmem((NZ, 32, D), BF16)] * 2,
        *[vmem((NY, 32, 128), BF16)] * 2,
        *[vmem((16, 2, 16, 128), BF16)] * 4,
        *[vmem((NY, 32, 128), BF16)] * 2,
        *[vmem((NZ, 32, D), BF16)] * 2,
        vmem((NX, 16, D), BF16),
        vmem((CH, 128), BF16),
        vmem((NY, CH, 128), BF16),
        vmem((3, NG, CH, D), BF16),
        vmem((3, 3 * D, D), BF16),
        vmem((3, D, D), BF16),
        vmem((4 * D, D), F32),
        vmem((CH, 128), F32),
        *save * 3,
        dma((6,)),
        dma((6,)),
        dma,
        dma,
        dma((2,)),
        dma((3,)),
        dma((3,)),
        dma((3,)),
        dma((3, NZ)),
        dma((3,)),
        dma((3,)),
    ]
    block = volume.shape
    whole = pl.BlockSpec(memory_space=pltpu.VMEM)
    got = pl.pallas_call(
        kernel,
        out_shape=jax.ShapeDtypeStruct((8, 16, D), BF16),
        in_specs=[whole] * 4,
        out_specs=whole,
        scratch_shapes=scratch,
        compiler_params=pltpu.CompilerParams(
            collective_id=0, has_side_effects=True, vmem_limit_bytes=48 * 1024 * 1024
        ),
    )(
        volume.reshape(8, 16, D),
        cotangent.reshape(8, 16, D),
        w_project.reshape(3 * ROWS, QKV),
        w_output.reshape(3 * ROWS, OUT),
    )
    return got.reshape(block)


def solution(mesh):
    return jax.shard_map(
        local,
        mesh=mesh,
        in_specs=(
            P("gz", "gy", "gx", None),
            P("gz", "gy", "gx", None),
            P(None, "gy", ("gz", "gx")),
            P(None, "gy", ("gz", "gx")),
        ),
        out_specs=P("gz", "gy", "gx", None),
        check_vma=False,
    )
```

```python
import functools

import jax
import jax.numpy as jnp
from jax import lax
from jax.experimental import pallas as pl
from jax.experimental.pallas import tpu as pltpu
from jax.sharding import PartitionSpec as P

MESH = pl.DeviceIdType.MESH
F32 = jnp.float32
BF16 = jnp.bfloat16
HEADS = 6
HEAD = 64
D = 384
EPS = 1e-06
TOK = 128
NZ, NY, NX = 4, 16, 8
NG = NZ * NX
QKV = 36
OUT = 12
CH = QKV + OUT
ROWS = 24


def dot(a, b, ca, cb):
    return lax.dot_general(a, b, (((ca,), (cb,)), ((), ())), preferred_element_type=F32)


def roll4(x):
    return pltpu.roll(x, 4, x.ndim - 2)


def low_half(shape):
    return lax.broadcasted_iota(jnp.int32, shape, len(shape) - 2) % 8 < 4


def swap_halves(u, v):
    low = low_half(u.shape)
    return jnp.where(low, u, roll4(v)), jnp.where(low, roll4(u), v)


def forward(stream, w_t, wo_t, mask, save):
    inv = lax.rsqrt(jnp.mean(stream * stream, axis=-1, keepdims=True) + EPS)
    normed = (stream * inv).astype(BF16)
    packed = dot(w_t, normed, 1, 1)
    heads = packed.reshape(3, HEADS, HEAD, TOK)
    inv_qk = lax.rsqrt(jnp.mean(heads[:2] * heads[:2], axis=2, keepdims=True) + EPS)
    qk = (heads[:2] * inv_qk).astype(BF16)
    val = heads[2].astype(BF16)
    mixed = []
    for h in range(HEADS):
        scores = dot(qk[1, h], qk[0, h], 0, 0) * (HEAD**-0.5)
        powers = jnp.exp(scores)
        if mask is not None:
            powers = jnp.where(mask, powers, 0.0)
        attn = (powers / jnp.sum(powers, axis=0, keepdims=True)).astype(BF16)
        save["attn"][h] = attn
        mixed.append(dot(val[h], attn, 1, 0).astype(BF16))
    mixed = jnp.concatenate(mixed, axis=0)
    save["inv"][...] = inv
    save["normed"][...] = normed
    save["inv_qk"][...] = inv_qk.reshape(2 * HEADS, 1, TOK)
    save["qkv"][: 2 * HEADS] = qk.reshape(2 * HEADS, HEAD, TOK)
    save["qkv"][2 * HEADS :] = val
    if wo_t is None:
        return None
    return stream + dot(wo_t, mixed, 1, 0).T


def backward(grad, w_t, wo_t, save):
    mixed_grad = dot(grad, wo_t, 1, 0).T.astype(BF16)
    packed_grad = [None] * (3 * HEADS)
    for h in range(HEADS):
        q, k, v = save["qkv"][h], save["qkv"][HEADS + h], save["qkv"][2 * HEADS + h]
        attn = save["attn"][h]
        attn32 = attn.astype(F32)
        d_mixed = mixed_grad[h * HEAD : (h + 1) * HEAD]
        d_attn = dot(v, d_mixed, 0, 0)
        d_v = dot(d_mixed, attn, 1, 1)
        d_scores = attn32 * (d_attn - jnp.sum(d_attn * attn32, axis=0, keepdims=True))
        d_scores = (d_scores * (HEAD**-0.5)).astype(BF16)
        d_q = dot(k, d_scores, 1, 0)
        d_k = dot(q, d_scores, 1, 1)
        for at, unit, d_unit in ((h, q, d_q), (HEADS + h, k, d_k)):
            unit32 = unit.astype(F32)
            proj = jnp.mean(d_unit * unit32, axis=0, keepdims=True)
            packed_grad[at] = (save["inv_qk"][at] * (d_unit - unit32 * proj)).astype(BF16)
        packed_grad[2 * HEADS + h] = d_v.astype(BF16)
    packed_grad = jnp.concatenate(packed_grad, axis=0)
    d_normed = dot(packed_grad, w_t, 0, 0)
    normed32 = save["normed"][...].astype(F32)
    proj = jnp.mean(d_normed * normed32, axis=-1, keepdims=True)
    return grad.astype(F32) + save["inv"][...] * (d_normed - normed32 * proj)


def line_mask(lines):
    row = lax.broadcasted_iota(jnp.int32, (TOK, TOK), 0)
    col = lax.broadcasted_iota(jnp.int32, (TOK, TOK), 1)
    return row % lines == col % lines


def split_home(block, out):
    x = block.astype(F32).reshape(4, 2, 2, 8, D)
    for half in range(2):
        low, high = swap_halves(x[:, 0, half], x[:, 1, half])
        out[2 * half] = low.reshape(32, D).astype(BF16)
        out[2 * half + 1] = high.reshape(32, D).astype(BF16)


def join_home(got, out):
    for half in range(2):
        u = got[2 * half].astype(F32).reshape(4, 8, D)
        v = got[2 * half + 1].astype(F32).reshape(4, 8, D)
        low, high = swap_halves(u, v)
        for m in range(4):
            out[2 * m, 8 * half : 8 * half + 8] = low[m].astype(BF16)
            out[2 * m + 1, 8 * half : 8 * half + 8] = high[m].astype(BF16)


def pack8(x, out):
    x = x.reshape(NY, 8, D)
    out[:, 0:16] = jnp.concatenate([x[:, :, 0:128], x[:, :, 128:256]], axis=1).astype(BF16)
    out[:, 16:32] = jnp.concatenate([x[:, :, 256:384], x[:, :, 256:384]], axis=1).astype(BF16)


def unpack8(got):
    x = got[...].astype(F32)
    return jnp.concatenate([x[:, 0:8], x[:, 8:16], x[:, 16:24]], axis=2).reshape(TOK, D)


def pack4(x, out):
    x = x.reshape(16, 8, D)
    first, second, third = x[:, :, 0:128], x[:, :, 128:256], x[:, :, 256:384]
    low, high = swap_halves(first, second)
    out[:, 0] = jnp.concatenate([low, third], axis=1).astype(BF16)
    out[:, 1] = jnp.concatenate([high, roll4(third)], axis=1).astype(BF16)


def unpack4(got):
    even, odd = got[:, 0].astype(F32), got[:, 1].astype(F32)
    first, second = swap_halves(even[:, 0:8], odd[:, 0:8])
    third = swap_halves(even[:, 8:16], odd[:, 8:16])[0]
    return jnp.concatenate([first, second, third], axis=2).reshape(TOK, D)


def own_chunk(w_ref, wo_ref, stage):
    rows = 3 * ROWS
    eye = (
        lax.broadcasted_iota(jnp.int32, (rows, 128), 0) == lax.broadcasted_iota(jnp.int32, (rows, 128), 1)
    ).astype(F32)
    block = jnp.concatenate([w_ref[i].astype(F32) for i in range(3)], axis=0).astype(BF16)
    stage[0:QKV] = dot(block, eye.astype(BF16), 0, 0)
    stage[QKV:CH] = sum(dot(wo_ref[i], eye[ROWS * i : ROWS * (i + 1)].astype(BF16), 1, 0) for i in range(3))
    return stage[...].astype(BF16)


def join_features(parts, layer):
    lane = lax.broadcasted_iota(jnp.int32, (CH, 128), 1)
    tiles = []
    for t in range(3):
        tile = None
        for g in range(NY):
            start = ROWS * g - 128 * t
            if start + ROWS <= 0 or start >= 128:
                continue
            piece = pltpu.roll(parts[g], (start - ROWS * layer) % 128, 1)
            tile = piece if tile is None else jnp.where(lane >= start, piece, tile)
        tiles.append(tile)
    return jnp.concatenate(tiles, axis=1)


def slot_of(unit):
    return (unit % 2) * 16 + (unit // 8) * 4 + (unit % 8) // 2


def compact(gathered, layer, w_t, wo_t, stage):
    for unit in range(NG):
        chunk = gathered[layer, slot_of(unit)].astype(F32)
        stage[QKV * unit : QKV * (unit + 1)] = chunk[:QKV]
        stage[3 * D + OUT * unit : 3 * D + OUT * (unit + 1)] = chunk[QKV:]
    w_t[layer] = stage[: 3 * D].astype(BF16)
    wo_t[layer] = stage[3 * D :].astype(BF16)


def kernel(
    vol_hbm, cot_hbm, w_hbm, wo_hbm, out,
    vol, w_in, wo_in,
    h1s, h1r, h2s, h2r, h3s, h3r, g3s, g3r, g2s, g2r, g1s, g1r, cotr,
    wparts, gathered, w_t, wo_t, wstage, cstage,
    *rest,
):
    saves = []
    for i in range(3):
        a, b, c, d, e = rest[5 * i : 5 * i + 5]
        saves.append(dict(attn=a, inv=b, normed=c, inv_qk=d, qkv=e))
    load_sems, a2a_send, a2a_recv, cot_send, cot_recv, w_sems, wd_send, wd_recv, wx_recv, wc_send, wc_recv = rest[15:]
    gz, gy, gx = lax.axis_index("gz"), lax.axis_index("gy"), lax.axis_index("gx")
    core, ylo = gx % 2, gx // 2
    line = ((gz + NZ - 1) % NZ) * NX + gx
    column = gx * NZ + gz

    loads = [
        pltpu.make_async_copy(src, dst, load_sems.at[i])
        for i, (src, dst) in enumerate(((w_hbm, w_in), (wo_hbm, wo_in), (vol_hbm, vol)))
    ]
    for load in loads:
        load.start()

    def line_owner(d):
        return (d // NX + 1) % NZ, d % NX

    def column_owner(s):
        return s % NZ, s // NZ

    def send(src, dst, ssem, rsem, to):
        pltpu.make_async_remote_copy(
            src_ref=src, dst_ref=dst, send_sem=ssem, recv_sem=rsem, device_id=to, device_id_type=MESH
        ).start()

    def drain(ref, sem):
        pltpu.make_async_copy(ref, ref, sem).wait()

    def each(count, body):
        lax.fori_loop(0, count, lambda k, c: (body(k), c)[1], 0)

    barrier = pltpu.get_barrier_semaphore()

    def greet(to):
        pl.semaphore_signal(barrier, inc=1, device_id=to, device_id_type=MESH)

    each(NY - 1, lambda k: greet((gz, (gy + 1 + k) % NY, gx)))

    def greet_line(k):
        s = (column + 1 + k) % NG
        z, x = column_owner(s)
        greet((z, gy, x))

    each(NG - 1, greet_line)
    each(NX, lambda k: greet((gy // 4, line // 2, k)))

    loads[0].wait()
    loads[1].wait()
    wparts[gy] = own_chunk(w_in, wo_in, cstage)
    pl.semaphore_wait(barrier, NY - 1 + NG - 1 + 8)

    each(
        NY - 1,
        lambda k: send(
            wparts.at[gy], wparts.at[gy], w_sems.at[0], w_sems.at[1], (gz, (gy + 1 + k) % NY, gx)
        ),
    )

    def gz_exchange(src, dst, n):
        def body(k):
            to = (gz + 1 + k) % NZ
            send(src.at[to], dst.at[gz], a2a_send.at[n], a2a_recv.at[n], (to, gy, gx))

        each(NZ - 1, body)
        pltpu.make_async_copy(src.at[gz], dst.at[gz], a2a_recv.at[n]).start()

    def gy_exchange(src, dst, n):
        def body(k):
            to = (gy + 1 + k) % NY
            send(src.at[to], dst.at[gy], a2a_send.at[n], a2a_recv.at[n], (gz, to, gx))

        each(NY - 1, body)
        pltpu.make_async_copy(src.at[gy], dst.at[gy], a2a_recv.at[n]).start()

    loads[2].wait()
    split_home(vol[...], h1s)
    gz_exchange(h1s, h1r, 0)

    drain(wparts.at[pl.ds(0, NY - 1)], w_sems.at[1])
    parts = wparts[...].astype(F32)
    own = gz * 4 + ylo
    sibling = (gz, gy, gx + 1 - 2 * core)

    def piece(layer, at):
        return gathered.at[layer, core * 16 + at]

    def run4(layer, z):
        return gathered.at[layer, pl.ds(core * 16 + z * 4, 4)]

    def send_y(layer):
        def body(k):
            to = (ylo + 1 + k) % 4
            block = piece(layer, own)
            send(block, block, wd_send.at[layer], wd_recv.at[layer, own], (gz, gy, to * 2 + core))

        each(3, body)

    def send_x(layer, block, sem):
        each(3, lambda k: send(block, block, wd_send.at[layer], sem, ((gz + 1 + k) % NZ, gy, gx)))

    def send_core(layer, block):
        send(block, block, wc_send.at[layer], wc_recv.at[layer], sibling)

    gathered[0, core * 16 + own] = join_features(parts, 0).astype(BF16)
    send_y(0)
    send_x(0, piece(0, own), wd_recv.at[0, own])
    send_core(0, piece(0, own))
    for layer in (1, 2):
        gathered[layer, core * 16 + own] = join_features(parts, layer).astype(BF16)

    def pass_y(k):
        at = gz * 4 + (ylo + 1 + k) % 4
        block = piece(0, at)
        drain(block, wd_recv.at[0, at])
        send_x(0, block, wd_recv.at[0, at])
        send_core(0, block)

    each(3, pass_y)
    send_y(1)
    send_y(2)

    def pass_x(k):
        at = ((gz + 1 + k % 3) % NZ) * 4 + (ylo + k // 3) % 4
        block = piece(0, at)
        drain(block, wd_recv.at[0, at])
        send_core(0, block)

    each(12, pass_x)

    def spread(layer):
        def wait_y(k):
            at = gz * 4 + (ylo + 1 + k) % 4
            drain(piece(layer, at), wd_recv.at[layer, at])

        each(3, wait_y)
        block = run4(layer, gz)
        send_x(layer, block, wx_recv.at[layer, gz])
        send_core(layer, block)

    def pass_runs(layer):
        def body(k):
            z = (gz + 1 + k) % NZ
            block = run4(layer, z)
            drain(block, wx_recv.at[layer, z])
            send_core(layer, block)

        each(3, body)

    def finish_weights(layer):
        drain(gathered.at[layer, pl.ds(0, 16)], wc_recv.at[layer])
        compact(gathered, layer, w_t, wo_t, wstage)

    spread(1)

    def send_cot(k):
        z, x = line_owner(2 * gy + k % 2)
        send(cot_hbm.at[k], cotr.at[gx], cot_send, cot_recv, (z, 4 * gz + k // 2, x))

    each(8, send_cot)

    finish_weights(0)
    drain(h1r, a2a_recv.at[0])
    depth_mask = line_mask(4)
    x = h1r[...].reshape(TOK, D).astype(F32)
    x = forward(x, w_t[0], wo_t[0], depth_mask, saves[0])
    pack8(x, h2s)
    gy_exchange(h2s, h2r, 1)

    spread(2)
    pass_runs(1)
    finish_weights(1)
    drain(h2r, a2a_recv.at[1])
    row_mask = line_mask(8)
    x = forward(unpack8(h2r), w_t[1], wo_t[1], row_mask, saves[1])
    pack4(x, h3s)

    def line_exchange(src, dst, n):
        def body(k):
            d = (line + 1 + k) % NG
            z, x = line_owner(d)
            send(src.at[d // 2, d % 2], dst.at[column // 2, column % 2], a2a_send.at[n], a2a_recv.at[n], (z, gy, x))

        each(NG - 1, body)
        pltpu.make_async_copy(
            src.at[line // 2, line % 2], dst.at[column // 2, column % 2], a2a_recv.at[n]
        ).start()

    def column_exchange(src, dst, n):
        def body(k):
            s = (column + 1 + k) % NG
            z, x = column_owner(s)
            send(src.at[s // 2, s % 2], dst.at[line // 2, line % 2], a2a_send.at[n], a2a_recv.at[n], (z, gy, x))

        each(NG - 1, body)
        pltpu.make_async_copy(
            src.at[column // 2, column % 2], dst.at[line // 2, line % 2], a2a_recv.at[n]
        ).start()

    line_exchange(h3s, h3r, 2)

    pass_runs(2)
    finish_weights(2)
    drain(cotr, cot_recv)
    drain(h3r, a2a_recv.at[2])
    forward(unpack4(h3r), w_t[2], None, None, saves[2])
    g = backward(cotr[...].reshape(TOK, D), w_t[2], wo_t[2], saves[2])
    pack4(g, g3s)
    column_exchange(g3s, g3r, 3)

    drain(g3r, a2a_recv.at[3])
    g = backward(unpack4(g3r).astype(BF16), w_t[1], wo_t[1], saves[1])
    pack8(g, g2s)
    gy_exchange(g2s, g2r, 4)

    drain(g2r, a2a_recv.at[4])
    g = backward(unpack8(g2r).astype(BF16), w_t[0], wo_t[0], saves[0])
    g1s[...] = g.astype(BF16).reshape(NZ, 32, D)
    gz_exchange(g1s, g1r, 5)

    drain(wparts.at[pl.ds(0, NY - 1)], w_sems.at[0])
    drain(h1r.at[pl.ds(0, NZ - 1)], a2a_send.at[0])
    drain(cotr, cot_send)
    for layer in range(3):
        drain(gathered.at[layer, pl.ds(0, 15)], wd_send.at[layer])
        drain(gathered.at[layer, pl.ds(0, 16)], wc_send.at[layer])
    for n, ref in ((1, h2r), (4, g2r)):
        drain(ref.at[pl.ds(0, NY - 1)], a2a_send.at[n])
    for n, ref in ((2, h3r), (3, g3r)):
        drain(ref.at[pl.ds(0, 15)], a2a_send.at[n])
        drain(ref.at[15, pl.ds(0, 1)], a2a_send.at[n])
    drain(g1r.at[pl.ds(0, NZ - 1)], a2a_send.at[5])

    drain(g1r, a2a_recv.at[5])
    join_home(g1r, out)


def local(volume, cotangent, w_project, w_output):
    vmem = pltpu.VMEM
    save = [
        vmem((HEADS, TOK, TOK), BF16),
        vmem((TOK, 1), F32),
        vmem((TOK, D), BF16),
        vmem((2 * HEADS, 1, TOK), F32),
        vmem((3 * HEADS, HEAD, TOK), BF16),
    ]
    dma = pltpu.SemaphoreType.DMA
    scratch = [
        vmem((8, 16, D), BF16),
        vmem((3, ROWS, QKV), BF16),
        vmem((3, OUT, ROWS), BF16),
        *[vmem((NZ, 32, D), BF16)] * 2,
        *[vmem((NY, 32, 128), BF16)] * 2,
        *[vmem((16, 2, 16, 128), BF16)] * 4,
        *[vmem((NY, 32, 128), BF16)] * 2,
        *[vmem((NZ, 32, D), BF16)] * 2,
        vmem((NX, 16, D), BF16),
        vmem((NY, CH, 128), BF16),
        vmem((3, NG, CH, D), BF16),
        vmem((3, 3 * D, D), BF16),
        vmem((3, D, D), BF16),
        vmem((4 * D, D), F32),
        vmem((CH, 128), F32),
        *save * 3,
        dma((3,)),
        dma((6,)),
        dma((6,)),
        dma,
        dma,
        dma((2,)),
        dma((3,)),
        dma((3, 16)),
        dma((3, NZ)),
        dma((3,)),
        dma((3,)),
    ]
    block = volume.shape
    whole = pl.BlockSpec(memory_space=pltpu.VMEM)
    got = pl.pallas_call(
        kernel,
        out_shape=jax.ShapeDtypeStruct((8, 16, D), BF16),
        in_specs=[pl.BlockSpec(memory_space=pltpu.HBM)] * 4,
        out_specs=whole,
        scratch_shapes=scratch,
        compiler_params=pltpu.CompilerParams(
            collective_id=0, has_side_effects=True, vmem_limit_bytes=63_400_000
        ),
    )(
        volume.reshape(8, 16, D),
        cotangent.reshape(8, 16, D),
        w_project,
        jnp.swapaxes(w_output, 1, 2),
    )
    return got.reshape(block)


def solution(mesh):
    return jax.shard_map(
        local,
        mesh=mesh,
        in_specs=(
            P("gz", "gy", "gx", None),
            P("gz", "gy", "gx", None),
            P(None, "gy", ("gz", "gx")),
            P(None, "gy", ("gz", "gx")),
        ),
        out_specs=P("gz", "gy", "gx", None),
        check_vma=False,
    )
```

```python
import functools

import jax
import jax.numpy as jnp
from jax import lax
from jax.experimental import pallas as pl
from jax.experimental.pallas import tpu as pltpu
from jax.sharding import PartitionSpec as P

MESH = pl.DeviceIdType.MESH
F32 = jnp.float32
BF16 = jnp.bfloat16
HEADS = 6
HEAD = 64
D = 384
EPS = 1e-06
TOK = 128
NZ, NY, NX = 4, 16, 8
NG = NZ * NX
QKV = 36
OUT = 12
CH = QKV + OUT
ROWS = 24


def dot(a, b, ca, cb):
    return lax.dot_general(a, b, (((ca,), (cb,)), ((), ())), preferred_element_type=F32)


def roll4(x):
    return pltpu.roll(x, 4, x.ndim - 2)


def low_half(shape):
    return lax.broadcasted_iota(jnp.int32, shape, len(shape) - 2) % 8 < 4


def swap_halves(u, v):
    low = low_half(u.shape)
    return jnp.where(low, u, roll4(v)), jnp.where(low, roll4(u), v)


def place(block):
    return (block % 2) * 8 + block // 2


def order_matrix():
    row = lax.broadcasted_iota(jnp.int32, (D, D), 0)
    col = lax.broadcasted_iota(jnp.int32, (D, D), 1)
    block = col // ROWS
    source = ((block % 8) * 2 + block // 8) * ROWS + col % ROWS
    return (row == source).astype(F32).astype(BF16)


def to_order(x):
    blocks = [x[ROWS * b : ROWS * (b + 1)] for b in range(NY)]
    return jnp.concatenate([blocks[(p % 8) * 2 + p // 8] for p in range(NY)], axis=0)


def from_order(x):
    blocks = [x[ROWS * p : ROWS * (p + 1)] for p in range(NY)]
    return jnp.concatenate([blocks[place(b)] for b in range(NY)], axis=0)


def forward(stream, w_t, wo_t, mask, save):
    inv = lax.rsqrt(jnp.mean(stream * stream, axis=-1, keepdims=True) + EPS)
    normed = (stream * inv).astype(BF16)
    packed = dot(w_t, normed, 1, 1)
    heads = packed.reshape(3, HEADS, HEAD, TOK)
    inv_qk = lax.rsqrt(jnp.mean(heads[:2] * heads[:2], axis=2, keepdims=True) + EPS)
    qk = (heads[:2] * inv_qk).astype(BF16)
    val = heads[2].astype(BF16)
    mixed = []
    for h in range(HEADS):
        scores = dot(qk[1, h], qk[0, h], 0, 0) * (HEAD**-0.5)
        powers = jnp.exp(scores)
        if mask is not None:
            powers = jnp.where(mask, powers, 0.0)
        attn = (powers / jnp.sum(powers, axis=0, keepdims=True)).astype(BF16)
        save["attn"][h] = attn
        mixed.append(dot(val[h], attn, 1, 0))
    mixed = to_order(jnp.concatenate(mixed, axis=0)).astype(BF16)
    save["inv"][...] = inv
    save["normed"][...] = normed
    save["inv_qk"][...] = inv_qk.reshape(2 * HEADS, 1, TOK)
    save["qkv"][: 2 * HEADS] = qk.reshape(2 * HEADS, HEAD, TOK)
    save["qkv"][2 * HEADS :] = val
    if wo_t is None:
        return None
    return stream + dot(wo_t, mixed, 1, 0).T


def backward(grad, w_t, wo_t, save):
    mixed_grad = from_order(dot(grad, wo_t, 1, 0).T).astype(BF16)
    packed_grad = [None] * (3 * HEADS)
    for h in range(HEADS):
        q, k, v = save["qkv"][h], save["qkv"][HEADS + h], save["qkv"][2 * HEADS + h]
        attn = save["attn"][h]
        attn32 = attn.astype(F32)
        d_mixed = mixed_grad[h * HEAD : (h + 1) * HEAD]
        d_attn = dot(v, d_mixed, 0, 0)
        d_v = dot(d_mixed, attn, 1, 1)
        d_scores = attn32 * (d_attn - jnp.sum(d_attn * attn32, axis=0, keepdims=True))
        d_scores = (d_scores * (HEAD**-0.5)).astype(BF16)
        d_q = dot(k, d_scores, 1, 0)
        d_k = dot(q, d_scores, 1, 1)
        for at, unit, d_unit in ((h, q, d_q), (HEADS + h, k, d_k)):
            unit32 = unit.astype(F32)
            proj = jnp.mean(d_unit * unit32, axis=0, keepdims=True)
            packed_grad[at] = (save["inv_qk"][at] * (d_unit - unit32 * proj)).astype(BF16)
        packed_grad[2 * HEADS + h] = d_v.astype(BF16)
    packed_grad = jnp.concatenate(packed_grad, axis=0)
    d_normed = dot(packed_grad, w_t, 0, 0)
    normed32 = save["normed"][...].astype(F32)
    proj = jnp.mean(d_normed * normed32, axis=-1, keepdims=True)
    return grad.astype(F32) + save["inv"][...] * (d_normed - normed32 * proj)


def line_mask(lines):
    row = lax.broadcasted_iota(jnp.int32, (TOK, TOK), 0)
    col = lax.broadcasted_iota(jnp.int32, (TOK, TOK), 1)
    return row % lines == col % lines


def split_home(block, out):
    x = block.astype(F32).reshape(4, 2, 2, 8, D)
    for half in range(2):
        low, high = swap_halves(x[:, 0, half], x[:, 1, half])
        out[2 * half] = low.reshape(32, D).astype(BF16)
        out[2 * half + 1] = high.reshape(32, D).astype(BF16)


def join_home(got, out):
    for half in range(2):
        u = got[2 * half].astype(F32).reshape(4, 8, D)
        v = got[2 * half + 1].astype(F32).reshape(4, 8, D)
        low, high = swap_halves(u, v)
        for m in range(4):
            out[2 * m, 8 * half : 8 * half + 8] = low[m].astype(BF16)
            out[2 * m + 1, 8 * half : 8 * half + 8] = high[m].astype(BF16)


def pack8(x, out):
    x = x.reshape(NY, 8, D)
    out[:, 0:16] = jnp.concatenate([x[:, :, 0:128], x[:, :, 128:256]], axis=1).astype(BF16)
    out[:, 16:32] = jnp.concatenate([x[:, :, 256:384], x[:, :, 256:384]], axis=1).astype(BF16)


def unpack8(got):
    x = got[...].astype(F32)
    return jnp.concatenate([x[:, 0:8], x[:, 8:16], x[:, 16:24]], axis=2).reshape(TOK, D)


def pack4(x, out):
    x = x.reshape(16, 8, D)
    first, second, third = x[:, :, 0:128], x[:, :, 128:256], x[:, :, 256:384]
    low, high = swap_halves(first, second)
    out[:, 0] = jnp.concatenate([low, third], axis=1).astype(BF16)
    out[:, 1] = jnp.concatenate([high, roll4(third)], axis=1).astype(BF16)


def unpack4(got):
    even, odd = got[:, 0].astype(F32), got[:, 1].astype(F32)
    first, second = swap_halves(even[:, 0:8], odd[:, 0:8])
    third = swap_halves(even[:, 8:16], odd[:, 8:16])[0]
    return jnp.concatenate([first, second, third], axis=2).reshape(TOK, D)


def own_chunk(w_ref, wo_ref, stage):
    rows = 3 * ROWS
    eye = (
        lax.broadcasted_iota(jnp.int32, (rows, 128), 0) == lax.broadcasted_iota(jnp.int32, (rows, 128), 1)
    ).astype(F32)
    block = jnp.concatenate([w_ref[i].astype(F32) for i in range(3)], axis=0).astype(BF16)
    stage[0:QKV] = dot(block, eye.astype(BF16), 0, 0)
    stage[QKV:CH] = sum(dot(wo_ref[i], eye[ROWS * i : ROWS * (i + 1)].astype(BF16), 1, 0) for i in range(3))
    return stage[...].astype(BF16)


def join_blocks(parts, pieces, tiles):
    lane = lax.broadcasted_iota(jnp.int32, (CH, 128), 1)
    joined = []
    for t in range(tiles):
        tile = None
        for n, (g, first) in enumerate(pieces):
            start = ROWS * n - 128 * t
            if start + ROWS <= 0 or start >= 128:
                continue
            piece = pltpu.roll(parts[g], (start - first) % 128, 1)
            tile = piece if tile is None else jnp.where(lane >= start, piece, tile)
        joined.append(tile)
    return joined


def half_roll(x):
    return pltpu.roll(x, 64, 1)


def join_halves(a, b):
    low = lax.broadcasted_iota(jnp.int32, (CH, 128), 1) < 64
    b0, b1 = half_roll(b[:, 0:128]), half_roll(b[:, 128:256])
    return jnp.concatenate([a[:, 0:128], jnp.where(low, a[:, 128:256], b0), jnp.where(low, b0, b1)], axis=1).astype(BF16)


def slot_of(unit):
    return (unit % 2) * 16 + (unit // 8) * 4 + (unit % 8) // 2


def compact(gathered, layer, w_t, wo_t, stage):
    for unit in range(NG):
        chunk = gathered[layer, slot_of(unit)].astype(F32)
        stage[QKV * unit : QKV * (unit + 1)] = chunk[:QKV]
        at = 3 * D + ROWS * place(unit // 2) + OUT * (unit % 2)
        stage[at : at + OUT] = chunk[QKV:]
    w_t[layer] = stage[: 3 * D].astype(BF16)
    wo_t[layer] = stage[3 * D :].astype(BF16)


def kernel(
    vol_hbm, cot_hbm, w_hbm, wo_hbm, out,
    vol, w_in, wo_in,
    h1s, h1r, h2s, h2r, h3s, h3r, g3s, g3r, g2s, g2r, g1s, g1r, cotr,
    order, wparts, ybuf, gathered, w_t, wo_t, wstage, cstage,
    *rest,
):
    saves = []
    for i in range(3):
        a, b, c, d, e = rest[5 * i : 5 * i + 5]
        saves.append(dict(attn=a, inv=b, normed=c, inv_qk=d, qkv=e))
    load_sems, a2a_send, a2a_recv, cot_send, cot_recv, w_sems, y_send, y_recv, x_send, x_first, x_recv, c_send, c_recv = rest[15:]
    gz, gy, gx = lax.axis_index("gz"), lax.axis_index("gy"), lax.axis_index("gx")
    core, ylo = gx % 2, gx // 2
    z, yhi = gy // 2, gy % 2
    y = yhi * 4 + ylo
    line = ((gz + NZ - 1) % NZ) * NX + gx
    column = gx * NZ + gz

    loads = [
        pltpu.make_async_copy(src, dst, load_sems.at[i])
        for i, (src, dst) in enumerate(((w_hbm, w_in), (wo_hbm, wo_in), (vol_hbm, vol)))
    ]
    for load in loads:
        load.start()

    def line_owner(d):
        return (d // NX + 1) % NZ, d % NX

    def column_owner(s):
        return s % NZ, s // NZ

    def send(src, dst, ssem, rsem, to):
        pltpu.make_async_remote_copy(
            src_ref=src, dst_ref=dst, send_sem=ssem, recv_sem=rsem, device_id=to, device_id_type=MESH
        ).start()

    def drain(ref, sem):
        pltpu.make_async_copy(ref, ref, sem).wait()

    def each(count, body):
        for k in range(count):
            body(k)

    barrier = pltpu.get_barrier_semaphore()

    def greet(to):
        pl.semaphore_signal(barrier, inc=1, device_id=to, device_id_type=MESH)

    def on_z(k):
        return gz, ((z + 1 + k) % 8) * 2 + yhi, gx

    def on_y(k):
        to = (y + 1 + k) % 8
        return gz, z * 2 + to // 4, (to % 4) * 2 + core

    def on_x(k):
        return (gz + 1 + k) % NZ, gy, gx

    sibling = (gz, gy, gx + 1 - 2 * core)
    each(7, lambda k: greet(on_z(k)))
    each(7, lambda k: greet(on_y(k)))
    each(3, lambda k: greet(on_x(k)))
    greet(sibling)

    loads[0].wait()
    loads[1].wait()
    wparts[z] = own_chunk(w_in, wo_in, cstage)
    pl.semaphore_wait(barrier, 18)

    each(7, lambda k: send(wparts.at[z], wparts.at[z], w_sems.at[0], w_sems.at[1], on_z(k)))

    def gz_exchange(src, dst, n):
        def body(k):
            to = (gz + 1 + k) % NZ
            send(src.at[to], dst.at[gz], a2a_send.at[n], a2a_recv.at[n], (to, gy, gx))

        each(NZ - 1, body)
        pltpu.make_async_copy(src.at[gz], dst.at[gz], a2a_recv.at[n]).start()

    def gy_exchange(src, dst, n):
        def body(k):
            to = (gy + 1 + k) % NY
            send(src.at[to], dst.at[gy], a2a_send.at[n], a2a_recv.at[n], (gz, to, gx))

        each(NY - 1, body)
        pltpu.make_async_copy(src.at[gy], dst.at[gy], a2a_recv.at[n]).start()

    loads[2].wait()
    order[...] = order_matrix()
    split_home(dot(vol[...].reshape(TOK, D), order[...], 1, 0).reshape(8, 16, D), h1s)
    gz_exchange(h1s, h1r, 0)

    drain(wparts.at[pl.ds(0, 7)], w_sems.at[1])
    parts = wparts[...].astype(F32)

    def send_y(layer):
        tiles = join_blocks(parts, [(g, ROWS * layer) for g in range(8)], 2)
        ybuf[layer, y] = jnp.concatenate(tiles, axis=1).astype(BF16)
        block = ybuf.at[layer, y]
        each(7, lambda k: send(block, block, y_send.at[layer], y_recv.at[layer, y], on_y(k)))

    send_y(0)

    def run4(layer, at):
        return gathered.at[layer, pl.ds(core * 16 + at * 4, 4)]

    def send_x(layer, block, sem):
        each(3, lambda k: send(block, block, x_send.at[layer], sem, on_x(k)))

    def send_core(layer, block):
        send(block, block, c_send.at[layer], c_recv.at[layer], sibling)

    def join_y(layer, u):
        for half in range(2):
            at = half * 4 + u

            @pl.when(at != y)
            def _(at=at):
                drain(ybuf.at[layer, at], y_recv.at[layer, at])

        at = core * 16 + gz * 4 + u
        gathered[layer, at] = join_halves(ybuf[layer, u].astype(F32), ybuf[layer, 4 + u].astype(F32))
        return gathered.at[layer, at]

    def pass_y(k):
        u = (ylo + k) % 4
        block = join_y(0, u)
        send_x(0, block, x_first.at[gz * 4 + u])
        send_core(0, block)

    each(4, pass_y)
    send_y(1)

    def pass_x(k):
        at = ((gz + 1 + k % 3) % NZ) * 4 + (ylo + k // 3) % 4
        block = gathered.at[0, core * 16 + at]
        drain(block, x_first.at[at])
        send_core(0, block)

    each(12, pass_x)

    def spread(layer):
        def body(k):
            join_y(layer, (ylo + k) % 4)

        each(4, body)
        block = run4(layer, gz)
        send_x(layer, block, x_recv.at[layer - 1, gz])
        send_core(layer, block)

    def pass_runs(layer):
        def body(k):
            at = (gz + 1 + k) % NZ
            block = run4(layer, at)
            drain(block, x_recv.at[layer - 1, at])
            send_core(layer, block)

        each(3, body)

    def finish_weights(layer):
        drain(gathered.at[layer, pl.ds(0, 16)], c_recv.at[layer])
        compact(gathered, layer, w_t, wo_t, wstage)

    spread(1)
    send_y(2)

    def send_cot(k):
        z, x = line_owner(2 * gy + k % 2)
        send(cot_hbm.at[k], cotr.at[gx], cot_send, cot_recv, (z, 4 * gz + k // 2, x))

    each(8, send_cot)

    finish_weights(0)
    drain(h1r, a2a_recv.at[0])
    depth_mask = line_mask(4)
    x = h1r[...].reshape(TOK, D).astype(F32)
    x = forward(x, w_t[0], wo_t[0], depth_mask, saves[0])
    pack8(x, h2s)
    gy_exchange(h2s, h2r, 1)

    spread(2)
    pass_runs(1)
    finish_weights(1)
    drain(h2r, a2a_recv.at[1])
    row_mask = line_mask(8)
    x = forward(unpack8(h2r), w_t[1], wo_t[1], row_mask, saves[1])
    pack4(x, h3s)

    def line_exchange(src, dst, n):
        def body(k):
            d = (line + 1 + k) % NG
            z, x = line_owner(d)
            send(src.at[d // 2, d % 2], dst.at[column // 2, column % 2], a2a_send.at[n], a2a_recv.at[n], (z, gy, x))

        each(NG - 1, body)
        pltpu.make_async_copy(
            src.at[line // 2, line % 2], dst.at[column // 2, column % 2], a2a_recv.at[n]
        ).start()

    def column_exchange(src, dst, n):
        def body(k):
            s = (column + 1 + k) % NG
            z, x = column_owner(s)
            send(src.at[s // 2, s % 2], dst.at[line // 2, line % 2], a2a_send.at[n], a2a_recv.at[n], (z, gy, x))

        each(NG - 1, body)
        pltpu.make_async_copy(
            src.at[column // 2, column % 2], dst.at[line // 2, line % 2], a2a_recv.at[n]
        ).start()

    line_exchange(h3s, h3r, 2)

    pass_runs(2)
    finish_weights(2)
    drain(cotr, cot_recv)
    g = dot(cotr[...].reshape(TOK, D), order[...], 1, 0).astype(BF16)
    drain(h3r, a2a_recv.at[2])
    forward(unpack4(h3r), w_t[2], None, None, saves[2])
    g = backward(g, w_t[2], wo_t[2], saves[2])
    pack4(g, g3s)
    column_exchange(g3s, g3r, 3)

    drain(g3r, a2a_recv.at[3])
    g = backward(unpack4(g3r).astype(BF16), w_t[1], wo_t[1], saves[1])
    pack8(g, g2s)
    gy_exchange(g2s, g2r, 4)

    drain(g2r, a2a_recv.at[4])
    g = backward(unpack8(g2r).astype(BF16), w_t[0], wo_t[0], saves[0])
    g1s[...] = dot(g.astype(BF16), order[...], 1, 1).astype(BF16).reshape(NZ, 32, D)
    gz_exchange(g1s, g1r, 5)

    drain(wparts.at[pl.ds(0, 7)], w_sems.at[0])
    drain(h1r.at[pl.ds(0, NZ - 1)], a2a_send.at[0])
    drain(cotr, cot_send)
    for layer in range(3):
        drain(ybuf.at[layer, pl.ds(0, 7)], y_send.at[layer])
        drain(gathered.at[layer, pl.ds(0, 12)], x_send.at[layer])
        drain(gathered.at[layer, pl.ds(0, 16)], c_send.at[layer])
    for n, ref in ((1, h2r), (4, g2r)):
        drain(ref.at[pl.ds(0, NY - 1)], a2a_send.at[n])
    for n, ref in ((2, h3r), (3, g3r)):
        drain(ref.at[pl.ds(0, 15)], a2a_send.at[n])
        drain(ref.at[15, pl.ds(0, 1)], a2a_send.at[n])
    drain(g1r.at[pl.ds(0, NZ - 1)], a2a_send.at[5])

    drain(g1r, a2a_recv.at[5])
    join_home(g1r, out)


def local(volume, cotangent, w_project, w_output):
    vmem = pltpu.VMEM
    save = [
        vmem((HEADS, TOK, TOK), BF16),
        vmem((TOK, 1), F32),
        vmem((TOK, D), BF16),
        vmem((2 * HEADS, 1, TOK), F32),
        vmem((3 * HEADS, HEAD, TOK), BF16),
    ]
    dma = pltpu.SemaphoreType.DMA
    scratch = [
        vmem((8, 16, D), BF16),
        vmem((3, ROWS, QKV), BF16),
        vmem((3, OUT, ROWS), BF16),
        *[vmem((NZ, 32, D), BF16)] * 2,
        *[vmem((NY, 32, 128), BF16)] * 2,
        *[vmem((16, 2, 16, 128), BF16)] * 4,
        *[vmem((NY, 32, 128), BF16)] * 2,
        *[vmem((NZ, 32, D), BF16)] * 2,
        vmem((NX, 16, D), BF16),
        vmem((D, D), BF16),
        vmem((8, CH, 128), BF16),
        vmem((3, 8, CH, 256), BF16),
        vmem((3, NG, CH, D), BF16),
        vmem((3, 3 * D, D), BF16),
        vmem((3, D, D), BF16),
        vmem((4 * D, D), F32),
        vmem((CH, 128), F32),
        *save * 3,
        dma((3,)),
        dma((6,)),
        dma((6,)),
        dma,
        dma,
        dma((2,)),
        dma((3,)),
        dma((3, 8)),
        dma((3,)),
        dma((16,)),
        dma((2, NZ)),
        dma((3,)),
        dma((3,)),
    ]
    block = volume.shape
    whole = pl.BlockSpec(memory_space=pltpu.VMEM)
    got = pl.pallas_call(
        kernel,
        out_shape=jax.ShapeDtypeStruct((8, 16, D), BF16),
        in_specs=[pl.BlockSpec(memory_space=pltpu.HBM)] * 4,
        out_specs=whole,
        scratch_shapes=scratch,
        compiler_params=pltpu.CompilerParams(
            collective_id=0, has_side_effects=True, vmem_limit_bytes=63_400_000
        ),
    )(
        volume.reshape(8, 16, D),
        cotangent.reshape(8, 16, D),
        w_project,
        jnp.swapaxes(w_output, 1, 2),
    )
    return got.reshape(block)


def solution(mesh):
    return jax.shard_map(
        local,
        mesh=mesh,
        in_specs=(
            P("gz", "gy", "gx", None),
            P("gz", "gy", "gx", None),
            P(None, "gy", ("gz", "gx")),
            P(None, "gy", ("gz", "gx")),
        ),
        out_specs=P("gz", "gy", "gx", None),
        check_vma=False,
    )
```

```python
import functools

import jax
import jax.numpy as jnp
from jax import lax
from jax.experimental import pallas as pl
from jax.experimental.pallas import tpu as pltpu
from jax.sharding import PartitionSpec as P

MESH = pl.DeviceIdType.MESH
F32 = jnp.float32
BF16 = jnp.bfloat16
HEADS = 6
HEAD = 64
D = 384
EPS = 1e-06
TOK = 128
NZ, NY, NX = 4, 16, 8
NG = NZ * NX
QKV = 36
OUT = 12
CH = QKV + OUT
ROWS = 24


def ring(d, n):
    return min(d, n - d)


FAR_GY = sorted(
    ((dz, dy) for dz in range(8) for dy in range(2) if dz or dy), key=lambda p: -(ring(p[0], 8) + 4 * p[1])
)
FAR_GX = sorted(
    ((dx, m, dc) for dx in range(4) for m in range(4) for dc in range(2) if dx or m or dc),
    key=lambda p: -(ring(p[0], 4) + p[1]),
)


def dot(a, b, ca, cb):
    return lax.dot_general(a, b, (((ca,), (cb,)), ((), ())), preferred_element_type=F32)


def roll4(x):
    return pltpu.roll(x, 4, x.ndim - 2)


def low_half(shape):
    return lax.broadcasted_iota(jnp.int32, shape, len(shape) - 2) % 8 < 4


def swap_halves(u, v):
    low = low_half(u.shape)
    return jnp.where(low, u, roll4(v)), jnp.where(low, roll4(u), v)


def place(block):
    return (block % 2) * 8 + block // 2


def order_matrix():
    row = lax.broadcasted_iota(jnp.int32, (D, D), 0)
    col = lax.broadcasted_iota(jnp.int32, (D, D), 1)
    block = col // ROWS
    source = ((block % 8) * 2 + block // 8) * ROWS + col % ROWS
    return (row == source).astype(F32).astype(BF16)


def to_order(x):
    blocks = [x[ROWS * b : ROWS * (b + 1)] for b in range(NY)]
    return jnp.concatenate([blocks[(p % 8) * 2 + p // 8] for p in range(NY)], axis=0)


def from_order(x):
    blocks = [x[ROWS * p : ROWS * (p + 1)] for p in range(NY)]
    return jnp.concatenate([blocks[place(b)] for b in range(NY)], axis=0)


def forward(stream, w_t, wo_t, mask, save):
    inv = lax.rsqrt(jnp.mean(stream * stream, axis=-1, keepdims=True) + EPS)
    normed = (stream * inv).astype(BF16)
    packed = dot(w_t, normed, 1, 1)
    heads = packed.reshape(3, HEADS, HEAD, TOK)
    inv_qk = lax.rsqrt(jnp.mean(heads[:2] * heads[:2], axis=2, keepdims=True) + EPS)
    qk = (heads[:2] * inv_qk).astype(BF16)
    val = heads[2].astype(BF16)
    mixed = []
    for h in range(HEADS):
        scores = dot(qk[1, h], qk[0, h], 0, 0) * (HEAD**-0.5)
        powers = jnp.exp(scores)
        if mask is not None:
            powers = jnp.where(mask, powers, 0.0)
        attn = (powers / jnp.sum(powers, axis=0, keepdims=True)).astype(BF16)
        save["attn"][h] = attn
        mixed.append(dot(val[h], attn, 1, 0))
    mixed = to_order(jnp.concatenate(mixed, axis=0)).astype(BF16)
    save["inv"][...] = inv
    save["normed"][...] = normed
    save["inv_qk"][...] = inv_qk.reshape(2 * HEADS, 1, TOK)
    save["qkv"][: 2 * HEADS] = qk.reshape(2 * HEADS, HEAD, TOK)
    save["qkv"][2 * HEADS :] = val
    if wo_t is None:
        return None
    return stream + dot(wo_t, mixed, 1, 0).T


def backward(grad, w_t, wo_t, save):
    mixed_grad = from_order(dot(grad, wo_t, 1, 0).T).astype(BF16)
    packed_grad = [None] * (3 * HEADS)
    for h in range(HEADS):
        q, k, v = save["qkv"][h], save["qkv"][HEADS + h], save["qkv"][2 * HEADS + h]
        attn = save["attn"][h]
        attn32 = attn.astype(F32)
        d_mixed = mixed_grad[h * HEAD : (h + 1) * HEAD]
        d_attn = dot(v, d_mixed, 0, 0)
        d_v = dot(d_mixed, attn, 1, 1)
        d_scores = attn32 * (d_attn - jnp.sum(d_attn * attn32, axis=0, keepdims=True))
        d_scores = (d_scores * (HEAD**-0.5)).astype(BF16)
        d_q = dot(k, d_scores, 1, 0)
        d_k = dot(q, d_scores, 1, 1)
        for at, unit, d_unit in ((h, q, d_q), (HEADS + h, k, d_k)):
            unit32 = unit.astype(F32)
            proj = jnp.mean(d_unit * unit32, axis=0, keepdims=True)
            packed_grad[at] = (save["inv_qk"][at] * (d_unit - unit32 * proj)).astype(BF16)
        packed_grad[2 * HEADS + h] = d_v.astype(BF16)
    packed_grad = jnp.concatenate(packed_grad, axis=0)
    d_normed = dot(packed_grad, w_t, 0, 0)
    normed32 = save["normed"][...].astype(F32)
    proj = jnp.mean(d_normed * normed32, axis=-1, keepdims=True)
    return grad.astype(F32) + save["inv"][...] * (d_normed - normed32 * proj)


def line_mask(lines):
    row = lax.broadcasted_iota(jnp.int32, (TOK, TOK), 0)
    col = lax.broadcasted_iota(jnp.int32, (TOK, TOK), 1)
    return row % lines == col % lines


def split_home(block, out):
    x = block.astype(F32).reshape(4, 2, 2, 8, D)
    for half in range(2):
        low, high = swap_halves(x[:, 0, half], x[:, 1, half])
        out[2 * half] = low.reshape(32, D).astype(BF16)
        out[2 * half + 1] = high.reshape(32, D).astype(BF16)


def join_home(got, out):
    for half in range(2):
        u = got[2 * half].astype(F32).reshape(4, 8, D)
        v = got[2 * half + 1].astype(F32).reshape(4, 8, D)
        low, high = swap_halves(u, v)
        for m in range(4):
            out[2 * m, 8 * half : 8 * half + 8] = low[m].astype(BF16)
            out[2 * m + 1, 8 * half : 8 * half + 8] = high[m].astype(BF16)


def pack8(x, out):
    x = x.reshape(NY, 8, D)
    out[:, 0:16] = jnp.concatenate([x[:, :, 0:128], x[:, :, 128:256]], axis=1).astype(BF16)
    out[:, 16:32] = jnp.concatenate([x[:, :, 256:384], x[:, :, 256:384]], axis=1).astype(BF16)


def unpack8(got):
    x = got[...].astype(F32)
    return jnp.concatenate([x[:, 0:8], x[:, 8:16], x[:, 16:24]], axis=2).reshape(TOK, D)


def pack4(x, out):
    x = x.reshape(16, 8, D)
    first, second, third = x[:, :, 0:128], x[:, :, 128:256], x[:, :, 256:384]
    low, high = swap_halves(first, second)
    out[:, 0] = jnp.concatenate([low, third], axis=1).astype(BF16)
    out[:, 1] = jnp.concatenate([high, roll4(third)], axis=1).astype(BF16)


def unpack4(got):
    even, odd = got[:, 0].astype(F32), got[:, 1].astype(F32)
    first, second = swap_halves(even[:, 0:8], odd[:, 0:8])
    third = swap_halves(even[:, 8:16], odd[:, 8:16])[0]
    return jnp.concatenate([first, second, third], axis=2).reshape(TOK, D)


def own_chunk(w_ref, wo_ref, stage):
    rows = 3 * ROWS
    eye = (
        lax.broadcasted_iota(jnp.int32, (rows, 128), 0) == lax.broadcasted_iota(jnp.int32, (rows, 128), 1)
    ).astype(F32)
    block = jnp.concatenate([w_ref[i].astype(F32) for i in range(3)], axis=0).astype(BF16)
    stage[0:QKV] = dot(block, eye.astype(BF16), 0, 0)
    stage[QKV:CH] = sum(dot(wo_ref[i], eye[ROWS * i : ROWS * (i + 1)].astype(BF16), 1, 0) for i in range(3))
    return stage[...].astype(BF16)


def join_blocks(parts, pieces, tiles):
    lane = lax.broadcasted_iota(jnp.int32, (CH, 128), 1)
    joined = []
    for t in range(tiles):
        tile = None
        for n, (g, first) in enumerate(pieces):
            start = ROWS * n - 128 * t
            if start + ROWS <= 0 or start >= 128:
                continue
            piece = pltpu.roll(parts[g], (start - first) % 128, 1)
            tile = piece if tile is None else jnp.where(lane >= start, piece, tile)
        joined.append(tile)
    return joined


def half_roll(x):
    return pltpu.roll(x, 64, 1)


def join_halves(a, b):
    low = lax.broadcasted_iota(jnp.int32, (CH, 128), 1) < 64
    b0, b1 = half_roll(b[:, 0:128]), half_roll(b[:, 128:256])
    return jnp.concatenate([a[:, 0:128], jnp.where(low, a[:, 128:256], b0), jnp.where(low, b0, b1)], axis=1).astype(BF16)


def slot_of(unit):
    return (unit % 2) * 16 + (unit // 8) * 4 + (unit % 8) // 2


def compact(gathered, layer, w_t, wo_t, stage):
    for unit in range(NG):
        chunk = gathered[layer, slot_of(unit)].astype(F32)
        stage[QKV * unit : QKV * (unit + 1)] = chunk[:QKV]
        at = 3 * D + ROWS * place(unit // 2) + OUT * (unit % 2)
        stage[at : at + OUT] = chunk[QKV:]
    w_t[layer] = stage[: 3 * D].astype(BF16)
    wo_t[layer] = stage[3 * D :].astype(BF16)


def kernel(
    vol_hbm, cot_hbm, w_hbm, wo_hbm, out,
    vol, w_in, wo_in,
    h1s, h1r, h2s, h2r, h3s, h3r, g3s, g3r, g2s, g2r, g1s, g1r, cotr,
    order, wparts, ybuf, gathered, w_t, wo_t, wstage, cstage,
    *rest,
):
    saves = []
    for i in range(3):
        a, b, c, d, e = rest[5 * i : 5 * i + 5]
        saves.append(dict(attn=a, inv=b, normed=c, inv_qk=d, qkv=e))
    load_sems, a2a_send, a2a_recv, cot_send, cot_recv, w_sems, y_send, y_recv, x_send, x_first, x_recv, c_send, c_recv = rest[15:]
    gz, gy, gx = lax.axis_index("gz"), lax.axis_index("gy"), lax.axis_index("gx")
    core, ylo = gx % 2, gx // 2
    z, yhi = gy // 2, gy % 2
    y = yhi * 4 + ylo
    line = ((gz + NZ - 1) % NZ) * NX + gx
    column = gx * NZ + gz

    loads = [
        pltpu.make_async_copy(src, dst, load_sems.at[i])
        for i, (src, dst) in enumerate(((w_hbm, w_in), (wo_hbm, wo_in), (vol_hbm, vol)))
    ]
    for load in loads:
        load.start()

    def line_owner(d):
        return (d // NX + 1) % NZ, d % NX

    def column_owner(s):
        return s % NZ, s // NZ

    def send(src, dst, ssem, rsem, to):
        pltpu.make_async_remote_copy(
            src_ref=src, dst_ref=dst, send_sem=ssem, recv_sem=rsem, device_id=to, device_id_type=MESH
        ).start()

    def drain(ref, sem):
        pltpu.make_async_copy(ref, ref, sem).wait()

    def each(count, body):
        for k in range(count):
            body(k)

    def far(k):
        dx, m, dc = FAR_GX[k]
        to = (ylo, ylo + 1 - 2 * (ylo % 2), (ylo + 2) % 4, 3 - ylo)[m]
        return (gz + dx) % NZ, to * 2 + (core + dc) % 2

    barrier = pltpu.get_barrier_semaphore()

    def greet(to):
        pl.semaphore_signal(barrier, inc=1, device_id=to, device_id_type=MESH)

    def on_z(k):
        return gz, ((z + 1 + k) % 8) * 2 + yhi, gx

    def on_y(k):
        to = (y + 1 + k) % 8
        return gz, z * 2 + to // 4, (to % 4) * 2 + core

    def on_x(k):
        return (gz + 1 + k) % NZ, gy, gx

    sibling = (gz, gy, gx + 1 - 2 * core)
    each(7, lambda k: greet(on_z(k)))
    each(7, lambda k: greet(on_y(k)))
    each(3, lambda k: greet(on_x(k)))
    greet(sibling)

    loads[0].wait()
    loads[1].wait()
    wparts[z] = own_chunk(w_in, wo_in, cstage)
    pl.semaphore_wait(barrier, 18)

    each(7, lambda k: send(wparts.at[z], wparts.at[z], w_sems.at[0], w_sems.at[1], on_z(k)))

    def gz_exchange(src, dst, n):
        def body(k):
            to = (gz + 1 + k) % NZ
            send(src.at[to], dst.at[gz], a2a_send.at[n], a2a_recv.at[n], (to, gy, gx))

        each(NZ - 1, body)
        pltpu.make_async_copy(src.at[gz], dst.at[gz], a2a_recv.at[n]).start()

    def gy_exchange(src, dst, n):
        def body(k):
            dz, dy = FAR_GY[k]
            to = ((z + dz) % 8) * 2 + (yhi + dy) % 2
            send(src.at[to], dst.at[gy], a2a_send.at[n], a2a_recv.at[n], (gz, to, gx))

        each(NY - 1, body)
        pltpu.make_async_copy(src.at[gy], dst.at[gy], a2a_recv.at[n]).start()

    loads[2].wait()
    order[...] = order_matrix()
    split_home(dot(vol[...].reshape(TOK, D), order[...], 1, 0).reshape(8, 16, D), h1s)
    gz_exchange(h1s, h1r, 0)

    drain(wparts.at[pl.ds(0, 7)], w_sems.at[1])
    parts = wparts[...].astype(F32)

    def send_y(layer):
        tiles = join_blocks(parts, [(g, ROWS * layer) for g in range(8)], 2)
        ybuf[layer, y] = jnp.concatenate(tiles, axis=1).astype(BF16)
        block = ybuf.at[layer, y]
        each(7, lambda k: send(block, block, y_send.at[layer], y_recv.at[layer, y], on_y(k)))

    send_y(0)

    def run4(layer, at):
        return gathered.at[layer, pl.ds(core * 16 + at * 4, 4)]

    def send_x(layer, block, sem):
        each(3, lambda k: send(block, block, x_send.at[layer], sem, on_x(k)))

    def send_core(layer, block):
        send(block, block, c_send.at[layer], c_recv.at[layer], sibling)

    def join_y(layer, u):
        for half in range(2):
            at = half * 4 + u

            @pl.when(at != y)
            def _(at=at):
                drain(ybuf.at[layer, at], y_recv.at[layer, at])

        at = core * 16 + gz * 4 + u
        gathered[layer, at] = join_halves(ybuf[layer, u].astype(F32), ybuf[layer, 4 + u].astype(F32))
        return gathered.at[layer, at]

    def pass_y(k):
        u = (ylo + k) % 4
        block = join_y(0, u)
        for way in (1, 3):
            send(block, block, x_send.at[0], x_first.at[gz * 4 + u], ((gz + way) % NZ, gy, gx))
        send_core(0, block)

    for k in range(4):
        pass_y(k)
        if k == 1:
            send_y(1)

    def pass_x(way, k):
        at = ((gz + way) % NZ) * 4 + (ylo + k) % 4
        block = gathered.at[0, core * 16 + at]
        drain(block, x_first.at[at])
        if (way, k) in ((3, 0), (3, 1), (1, 2), (1, 3)):
            send(block, block, x_send.at[0], x_first.at[at], ((gz - way + NZ) % NZ, gy, gx))
        send_core(0, block)

    for k in range(4):
        pass_x(3, k)
        pass_x(1, k)
    def spread(layer):
        def body(k):
            join_y(layer, (ylo + k) % 4)

        each(4, body)
        block = run4(layer, gz)
        send_x(layer, block, x_recv.at[layer - 1, gz])
        send_core(layer, block)

    spread(1)
    send_y(2)
    for k in range(4):
        pass_x(2, k)

    def pass_runs(layer):
        def body(k):
            at = (gz + 1 + k) % NZ
            block = run4(layer, at)
            drain(block, x_recv.at[layer - 1, at])
            send_core(layer, block)

        each(3, body)

    def finish_weights(layer):
        drain(gathered.at[layer, pl.ds(0, 16)], c_recv.at[layer])
        compact(gathered, layer, w_t, wo_t, wstage)


    def send_cot(k):
        z, x = line_owner(2 * gy + k % 2)
        send(cot_hbm.at[k], cotr.at[gx], cot_send, cot_recv, (z, 4 * gz + k // 2, x))

    each(8, send_cot)

    finish_weights(0)
    drain(h1r, a2a_recv.at[0])
    depth_mask = line_mask(4)
    x = h1r[...].reshape(TOK, D).astype(F32)
    x = forward(x, w_t[0], wo_t[0], depth_mask, saves[0])
    pack8(x, h2s)
    gy_exchange(h2s, h2r, 1)

    spread(2)
    pass_runs(1)
    finish_weights(1)
    drain(h2r, a2a_recv.at[1])
    row_mask = line_mask(8)
    x = forward(unpack8(h2r), w_t[1], wo_t[1], row_mask, saves[1])
    pack4(x, h3s)

    def line_exchange(src, dst, n):
        def body(k):
            z, x = far(k)
            d = ((z + NZ - 1) % NZ) * NX + x
            send(src.at[d // 2, d % 2], dst.at[column // 2, column % 2], a2a_send.at[n], a2a_recv.at[n], (z, gy, x))

        each(NG - 1, body)
        pltpu.make_async_copy(
            src.at[line // 2, line % 2], dst.at[column // 2, column % 2], a2a_recv.at[n]
        ).start()

    def column_exchange(src, dst, n):
        def body(k):
            z, x = far(k)
            s = x * NZ + z
            send(src.at[s // 2, s % 2], dst.at[line // 2, line % 2], a2a_send.at[n], a2a_recv.at[n], (z, gy, x))

        each(NG - 1, body)
        pltpu.make_async_copy(
            src.at[column // 2, column % 2], dst.at[line // 2, line % 2], a2a_recv.at[n]
        ).start()

    line_exchange(h3s, h3r, 2)

    pass_runs(2)
    finish_weights(2)
    drain(cotr, cot_recv)
    g = dot(cotr[...].reshape(TOK, D), order[...], 1, 0).astype(BF16)
    drain(h3r, a2a_recv.at[2])
    forward(unpack4(h3r), w_t[2], None, None, saves[2])
    g = backward(g, w_t[2], wo_t[2], saves[2])
    pack4(g, g3s)
    column_exchange(g3s, g3r, 3)

    drain(g3r, a2a_recv.at[3])
    g = backward(unpack4(g3r).astype(BF16), w_t[1], wo_t[1], saves[1])
    pack8(g, g2s)
    gy_exchange(g2s, g2r, 4)

    drain(g2r, a2a_recv.at[4])
    g = backward(unpack8(g2r).astype(BF16), w_t[0], wo_t[0], saves[0])
    g1s[...] = dot(g.astype(BF16), order[...], 1, 1).astype(BF16).reshape(NZ, 32, D)
    gz_exchange(g1s, g1r, 5)

    drain(wparts.at[pl.ds(0, 7)], w_sems.at[0])
    drain(h1r.at[pl.ds(0, NZ - 1)], a2a_send.at[0])
    drain(cotr, cot_send)
    for layer in range(3):
        drain(ybuf.at[layer, pl.ds(0, 7)], y_send.at[layer])
        drain(gathered.at[layer, pl.ds(0, 12)], x_send.at[layer])
        drain(gathered.at[layer, pl.ds(0, 16)], c_send.at[layer])
    for n, ref in ((1, h2r), (4, g2r)):
        drain(ref.at[pl.ds(0, NY - 1)], a2a_send.at[n])
    for n, ref in ((2, h3r), (3, g3r)):
        drain(ref.at[pl.ds(0, 15)], a2a_send.at[n])
        drain(ref.at[15, pl.ds(0, 1)], a2a_send.at[n])
    drain(g1r.at[pl.ds(0, NZ - 1)], a2a_send.at[5])

    drain(g1r, a2a_recv.at[5])
    join_home(g1r, out)


def local(volume, cotangent, w_project, w_output):
    vmem = pltpu.VMEM
    save = [
        vmem((HEADS, TOK, TOK), BF16),
        vmem((TOK, 1), F32),
        vmem((TOK, D), BF16),
        vmem((2 * HEADS, 1, TOK), F32),
        vmem((3 * HEADS, HEAD, TOK), BF16),
    ]
    dma = pltpu.SemaphoreType.DMA
    scratch = [
        vmem((8, 16, D), BF16),
        vmem((3, ROWS, QKV), BF16),
        vmem((3, OUT, ROWS), BF16),
        *[vmem((NZ, 32, D), BF16)] * 2,
        *[vmem((NY, 32, 128), BF16)] * 2,
        *[vmem((16, 2, 16, 128), BF16)] * 4,
        *[vmem((NY, 32, 128), BF16)] * 2,
        *[vmem((NZ, 32, D), BF16)] * 2,
        vmem((NX, 16, D), BF16),
        vmem((D, D), BF16),
        vmem((8, CH, 128), BF16),
        vmem((3, 8, CH, 256), BF16),
        vmem((3, NG, CH, D), BF16),
        vmem((3, 3 * D, D), BF16),
        vmem((3, D, D), BF16),
        vmem((4 * D, D), F32),
        vmem((CH, 128), F32),
        *save * 3,
        dma((3,)),
        dma((6,)),
        dma((6,)),
        dma,
        dma,
        dma((2,)),
        dma((3,)),
        dma((3, 8)),
        dma((3,)),
        dma((16,)),
        dma((2, NZ)),
        dma((3,)),
        dma((3,)),
    ]
    block = volume.shape
    whole = pl.BlockSpec(memory_space=pltpu.VMEM)
    got = pl.pallas_call(
        kernel,
        out_shape=jax.ShapeDtypeStruct((8, 16, D), BF16),
        in_specs=[pl.BlockSpec(memory_space=pltpu.HBM)] * 4,
        out_specs=whole,
        scratch_shapes=scratch,
        compiler_params=pltpu.CompilerParams(
            collective_id=0, has_side_effects=True, vmem_limit_bytes=50_000_000
        ),
    )(
        *(
            pltpu.with_memory_space_constraint(array, pltpu.HBM)
            for array in (
                volume.reshape(8, 16, D),
                cotangent.reshape(8, 16, D),
                w_project,
                jnp.swapaxes(w_output, 1, 2),
            )
        )
    )
    return got.reshape(block)


def solution(mesh):
    return jax.shard_map(
        local,
        mesh=mesh,
        in_specs=(
            P("gz", "gy", "gx", None),
            P("gz", "gy", "gx", None),
            P(None, "gy", ("gz", "gx")),
            P(None, "gy", ("gz", "gx")),
        ),
        out_specs=P("gz", "gy", "gx", None),
        check_vma=False,
    )
```

```python
import functools

import jax
import jax.numpy as jnp
from jax import lax
from jax.experimental import pallas as pl
from jax.experimental.pallas import tpu as pltpu
from jax.sharding import PartitionSpec as P

MESH = pl.DeviceIdType.MESH
F32 = jnp.float32
BF16 = jnp.bfloat16
HEADS = 6
HEAD = 64
D = 384
EPS = 1e-06
TOK = 128
NZ, NY, NX = 4, 16, 8
NG = NZ * NX
QKV = 36
OUT = 12
CH = QKV + OUT
ROWS = 24


def ring(d, n):
    return min(d, n - d)


FAR_GY = sorted(
    ((dz, dy) for dz in range(8) for dy in range(2) if dz or dy), key=lambda p: -(ring(p[0], 8) + 4 * p[1])
)
FAR_GX = sorted(
    ((dx, m, dc) for dx in range(4) for m in range(4) for dc in range(2) if dx or m or dc),
    key=lambda p: -(ring(p[0], 4) + p[1]),
)


def dot(a, b, ca, cb):
    return lax.dot_general(a, b, (((ca,), (cb,)), ((), ())), preferred_element_type=F32)


def roll4(x):
    return pltpu.roll(x, 4, x.ndim - 2)


def low_half(shape):
    return lax.broadcasted_iota(jnp.int32, shape, len(shape) - 2) % 8 < 4


def swap_halves(u, v):
    low = low_half(u.shape)
    return jnp.where(low, u, roll4(v)), jnp.where(low, roll4(u), v)


def place(block):
    return (block % 2) * 8 + block // 2


def order_matrix():
    row = lax.broadcasted_iota(jnp.int32, (D, D), 0)
    col = lax.broadcasted_iota(jnp.int32, (D, D), 1)
    block = col // ROWS
    source = ((block % 8) * 2 + block // 8) * ROWS + col % ROWS
    return (row == source).astype(F32).astype(BF16)


def to_order(x):
    blocks = [x[ROWS * b : ROWS * (b + 1)] for b in range(NY)]
    return jnp.concatenate([blocks[(p % 8) * 2 + p // 8] for p in range(NY)], axis=0)


def from_order(x):
    blocks = [x[ROWS * p : ROWS * (p + 1)] for p in range(NY)]
    return jnp.concatenate([blocks[place(b)] for b in range(NY)], axis=0)


def forward(stream, w_t, wo_t, mask, save):
    inv = lax.rsqrt(jnp.mean(stream * stream, axis=-1, keepdims=True) + EPS)
    normed = (stream * inv).astype(BF16)
    packed = dot(w_t, normed, 1, 1)
    heads = packed.reshape(3, HEADS, HEAD, TOK)
    inv_qk = lax.rsqrt(jnp.mean(heads[:2] * heads[:2], axis=2, keepdims=True) + EPS)
    qk = (heads[:2] * inv_qk).astype(BF16)
    val = heads[2].astype(BF16)
    each_head = range(HEADS)
    scores = [dot(qk[1, h], qk[0, h], 0, 0) * (HEAD**-0.5) for h in each_head]
    powers = [jnp.exp(x) for x in scores]
    if mask is not None:
        powers = [jnp.where(mask, x, 0.0) for x in powers]
    attn = [(x / jnp.sum(x, axis=0, keepdims=True)).astype(BF16) for x in powers]
    mixed = jnp.concatenate([dot(val[h], attn[h], 1, 0) for h in each_head], axis=0)
    result = None
    if wo_t is not None:
        result = stream + dot(wo_t, to_order(mixed).astype(BF16), 1, 0).T
    for h in each_head:
        save["attn"][h] = attn[h]
    save["inv"][...] = inv
    save["normed"][...] = normed
    save["inv_qk"][...] = inv_qk.reshape(2 * HEADS, 1, TOK)
    save["qkv"][: 2 * HEADS] = qk.reshape(2 * HEADS, HEAD, TOK)
    save["qkv"][2 * HEADS :] = val
    return result


def backward(grad, w_t, wo_t, save):
    mixed_grad = from_order(dot(grad, wo_t, 1, 0).T).astype(BF16)
    each_head = range(HEADS)
    q, k, v = ([save["qkv"][HEADS * i + h] for h in each_head] for i in range(3))
    attn = [save["attn"][h] for h in each_head]
    d_mixed = [mixed_grad[h * HEAD : (h + 1) * HEAD] for h in each_head]
    d_attn = [dot(v[h], d_mixed[h], 0, 0) for h in each_head]
    d_v = [dot(d_mixed[h], attn[h], 1, 1).astype(BF16) for h in each_head]
    d_scores = []
    for h in each_head:
        attn32 = attn[h].astype(F32)
        change = attn32 * (d_attn[h] - jnp.sum(d_attn[h] * attn32, axis=0, keepdims=True))
        d_scores.append((change * (HEAD**-0.5)).astype(BF16))
    d_q = [dot(k[h], d_scores[h], 1, 0) for h in each_head]
    d_k = [dot(q[h], d_scores[h], 1, 1) for h in each_head]
    packed_grad = []
    for at, (unit, d_unit) in enumerate(zip(q + k, d_q + d_k)):
        unit32 = unit.astype(F32)
        proj = jnp.mean(d_unit * unit32, axis=0, keepdims=True)
        packed_grad.append((save["inv_qk"][at] * (d_unit - unit32 * proj)).astype(BF16))
    packed_grad += d_v
    packed_grad = jnp.concatenate(packed_grad, axis=0)
    d_normed = dot(packed_grad, w_t, 0, 0)
    normed32 = save["normed"][...].astype(F32)
    proj = jnp.mean(d_normed * normed32, axis=-1, keepdims=True)
    return grad.astype(F32) + save["inv"][...] * (d_normed - normed32 * proj)


def line_mask(lines):
    row = lax.broadcasted_iota(jnp.int32, (TOK, TOK), 0)
    col = lax.broadcasted_iota(jnp.int32, (TOK, TOK), 1)
    return row % lines == col % lines


def split_home(block, out):
    x = block.astype(F32).reshape(4, 2, 2, 8, D)
    for half in range(2):
        low, high = swap_halves(x[:, 0, half], x[:, 1, half])
        out[2 * half] = low.reshape(32, D).astype(BF16)
        out[2 * half + 1] = high.reshape(32, D).astype(BF16)


def join_home(got, out):
    for half in range(2):
        u = got[2 * half].astype(F32).reshape(4, 8, D)
        v = got[2 * half + 1].astype(F32).reshape(4, 8, D)
        low, high = swap_halves(u, v)
        for m in range(4):
            out[2 * m, 8 * half : 8 * half + 8] = low[m].astype(BF16)
            out[2 * m + 1, 8 * half : 8 * half + 8] = high[m].astype(BF16)


def pack8(x, out):
    x = x.reshape(NY, 8, D)
    out[:, 0:16] = jnp.concatenate([x[:, :, 0:128], x[:, :, 128:256]], axis=1).astype(BF16)
    out[:, 16:32] = jnp.concatenate([x[:, :, 256:384], x[:, :, 256:384]], axis=1).astype(BF16)


def unpack8(got):
    x = got[...].astype(F32)
    return jnp.concatenate([x[:, 0:8], x[:, 8:16], x[:, 16:24]], axis=2).reshape(TOK, D)


def pack4(x, out):
    x = x.reshape(16, 8, D)
    first, second, third = x[:, :, 0:128], x[:, :, 128:256], x[:, :, 256:384]
    low, high = swap_halves(first, second)
    out[:, 0] = jnp.concatenate([low, third], axis=1).astype(BF16)
    out[:, 1] = jnp.concatenate([high, roll4(third)], axis=1).astype(BF16)


def unpack4(got):
    even, odd = got[:, 0].astype(F32), got[:, 1].astype(F32)
    first, second = swap_halves(even[:, 0:8], odd[:, 0:8])
    third = swap_halves(even[:, 8:16], odd[:, 8:16])[0]
    return jnp.concatenate([first, second, third], axis=2).reshape(TOK, D)


def own_chunk(w_ref, wo_ref, stage):
    rows = 3 * ROWS
    eye = (
        lax.broadcasted_iota(jnp.int32, (rows, 128), 0) == lax.broadcasted_iota(jnp.int32, (rows, 128), 1)
    ).astype(F32)
    block = jnp.concatenate([w_ref[i].astype(F32) for i in range(3)], axis=0).astype(BF16)
    stage[0:QKV] = dot(block, eye.astype(BF16), 0, 0)
    stage[QKV:CH] = sum(dot(wo_ref[i], eye[ROWS * i : ROWS * (i + 1)].astype(BF16), 1, 0) for i in range(3))
    return stage[...].astype(BF16)


def join_blocks(parts, pieces, tiles):
    lane = lax.broadcasted_iota(jnp.int32, (CH, 128), 1)
    joined = []
    for t in range(tiles):
        tile = None
        for n, (g, first) in enumerate(pieces):
            start = ROWS * n - 128 * t
            if start + ROWS <= 0 or start >= 128:
                continue
            piece = pltpu.roll(parts[g], (start - first) % 128, 1)
            tile = piece if tile is None else jnp.where(lane >= start, piece, tile)
        joined.append(tile)
    return joined


def half_roll(x):
    return pltpu.roll(x, 64, 1)


def join_halves(a, b):
    low = lax.broadcasted_iota(jnp.int32, (CH, 128), 1) < 64
    b0, b1 = half_roll(b[:, 0:128]), half_roll(b[:, 128:256])
    return jnp.concatenate([a[:, 0:128], jnp.where(low, a[:, 128:256], b0), jnp.where(low, b0, b1)], axis=1).astype(BF16)


def slot_of(unit):
    return (unit % 2) * 16 + (unit // 8) * 4 + (unit % 8) // 2


def compact(gathered, layer, w_t, wo_t, stage):
    for unit in range(NG):
        chunk = gathered[layer, slot_of(unit)].astype(F32)
        stage[QKV * unit : QKV * (unit + 1)] = chunk[:QKV]
        at = 3 * D + ROWS * place(unit // 2) + OUT * (unit % 2)
        stage[at : at + OUT] = chunk[QKV:]
    w_t[layer] = stage[: 3 * D].astype(BF16)
    wo_t[layer] = stage[3 * D :].astype(BF16)


def kernel(
    vol_hbm, cot_hbm, w_hbm, wo_hbm, out,
    vol, w_in, wo_in,
    h1s, h1r, h2s, h2r, h3s, h3r, g3s, g3r, g2s, g2r, g1s, g1r, cotr,
    order, wparts, ybuf, gathered, w_t, wo_t, wstage, cstage,
    *rest,
):
    saves = []
    for i in range(3):
        a, b, c, d, e = rest[5 * i : 5 * i + 5]
        saves.append(dict(attn=a, inv=b, normed=c, inv_qk=d, qkv=e))
    load_sems, a2a_send, a2a_recv, cot_send, cot_recv, w_sems, y_send, y_recv, x_send, x_first, x_recv, c_send, c_recv = rest[15:]
    gz, gy, gx = lax.axis_index("gz"), lax.axis_index("gy"), lax.axis_index("gx")
    core, ylo = gx % 2, gx // 2
    z, yhi = gy // 2, gy % 2
    y = yhi * 4 + ylo
    line = ((gz + NZ - 1) % NZ) * NX + gx
    column = gx * NZ + gz

    loads = [
        pltpu.make_async_copy(src, dst, load_sems.at[i])
        for i, (src, dst) in enumerate(((w_hbm, w_in), (wo_hbm, wo_in), (vol_hbm, vol)))
    ]
    for load in loads:
        load.start()

    def line_owner(d):
        return (d // NX + 1) % NZ, d % NX

    def column_owner(s):
        return s % NZ, s // NZ

    def send(src, dst, ssem, rsem, to):
        pltpu.make_async_remote_copy(
            src_ref=src, dst_ref=dst, send_sem=ssem, recv_sem=rsem, device_id=to, device_id_type=MESH
        ).start()

    def drain(ref, sem):
        pltpu.make_async_copy(ref, ref, sem).wait()

    def each(count, body):
        for k in range(count):
            body(k)

    def far(k):
        dx, m, dc = FAR_GX[k]
        to = (ylo, ylo + 1 - 2 * (ylo % 2), (ylo + 2) % 4, 3 - ylo)[m]
        return (gz + dx) % NZ, to * 2 + (core + dc) % 2

    barrier = pltpu.get_barrier_semaphore()

    def greet(to):
        pl.semaphore_signal(barrier, inc=1, device_id=to, device_id_type=MESH)

    def on_z(k):
        return gz, ((z + 1 + k) % 8) * 2 + yhi, gx

    def on_y(k):
        to = (y + 1 + k) % 8
        return gz, z * 2 + to // 4, (to % 4) * 2 + core

    def on_x(k):
        return (gz + 1 + k) % NZ, gy, gx

    sibling = (gz, gy, gx + 1 - 2 * core)
    each(7, lambda k: greet(on_z(k)))
    each(7, lambda k: greet(on_y(k)))
    each(3, lambda k: greet(on_x(k)))
    greet(sibling)

    loads[0].wait()
    loads[1].wait()
    wparts[z] = own_chunk(w_in, wo_in, cstage)
    pl.semaphore_wait(barrier, 18)

    each(7, lambda k: send(wparts.at[z], wparts.at[z], w_sems.at[0], w_sems.at[1], on_z(k)))

    def gz_exchange(src, dst, n):
        def body(k):
            to = (gz + 1 + k) % NZ
            send(src.at[to], dst.at[gz], a2a_send.at[n], a2a_recv.at[n], (to, gy, gx))

        each(NZ - 1, body)
        pltpu.make_async_copy(src.at[gz], dst.at[gz], a2a_recv.at[n]).start()

    def gy_exchange(src, dst, n):
        def body(k):
            dz, dy = FAR_GY[k]
            to = ((z + dz) % 8) * 2 + (yhi + dy) % 2
            send(src.at[to], dst.at[gy], a2a_send.at[n], a2a_recv.at[n], (gz, to, gx))

        each(NY - 1, body)
        pltpu.make_async_copy(src.at[gy], dst.at[gy], a2a_recv.at[n]).start()

    loads[2].wait()
    order[...] = order_matrix()
    split_home(dot(vol[...].reshape(TOK, D), order[...], 1, 0).reshape(8, 16, D), h1s)
    gz_exchange(h1s, h1r, 0)

    drain(wparts.at[pl.ds(0, 7)], w_sems.at[1])
    parts = wparts[...].astype(F32)

    def send_y(layer):
        tiles = join_blocks(parts, [(g, ROWS * layer) for g in range(8)], 2)
        ybuf[layer, y] = jnp.concatenate(tiles, axis=1).astype(BF16)
        block = ybuf.at[layer, y]
        each(7, lambda k: send(block, block, y_send.at[layer], y_recv.at[layer, y], on_y(k)))

    send_y(0)

    def run4(layer, at):
        return gathered.at[layer, pl.ds(core * 16 + at * 4, 4)]

    def send_x(layer, block, sem):
        each(3, lambda k: send(block, block, x_send.at[layer], sem, on_x(k)))

    def send_core(layer, block):
        send(block, block, c_send.at[layer], c_recv.at[layer], sibling)

    def join_y(layer, u):
        for half in range(2):
            at = half * 4 + u

            @pl.when(at != y)
            def _(at=at):
                drain(ybuf.at[layer, at], y_recv.at[layer, at])

        at = core * 16 + gz * 4 + u
        gathered[layer, at] = join_halves(ybuf[layer, u].astype(F32), ybuf[layer, 4 + u].astype(F32))
        return gathered.at[layer, at]

    def pass_y(k):
        u = (ylo + k) % 4
        block = join_y(0, u)
        for way in (1, 3):
            send(block, block, x_send.at[0], x_first.at[gz * 4 + u], ((gz + way) % NZ, gy, gx))
        send_core(0, block)

    for k in range(4):
        pass_y(k)
        if k == 1:
            send_y(1)

    def pass_x(way, k):
        at = ((gz + way) % NZ) * 4 + (ylo + k) % 4
        block = gathered.at[0, core * 16 + at]
        drain(block, x_first.at[at])
        if (way, k) in ((3, 0), (3, 1), (1, 2), (1, 3)):
            send(block, block, x_send.at[0], x_first.at[at], ((gz - way + NZ) % NZ, gy, gx))
        send_core(0, block)

    for k in range(4):
        pass_x(3, k)
        pass_x(1, k)
    def spread(layer):
        def body(k):
            join_y(layer, (ylo + k) % 4)

        each(4, body)
        block = run4(layer, gz)
        send_x(layer, block, x_recv.at[layer - 1, gz])
        send_core(layer, block)

    spread(1)
    send_y(2)
    for k in range(4):
        pass_x(2, k)

    def pass_runs(layer):
        def body(k):
            at = (gz + 1 + k) % NZ
            block = run4(layer, at)
            drain(block, x_recv.at[layer - 1, at])
            send_core(layer, block)

        each(3, body)

    def finish_weights(layer):
        drain(gathered.at[layer, pl.ds(0, 16)], c_recv.at[layer])
        compact(gathered, layer, w_t, wo_t, wstage)


    def send_cot(k):
        z, x = line_owner(2 * gy + k % 2)
        send(cot_hbm.at[k], cotr.at[gx], cot_send, cot_recv, (z, 4 * gz + k // 2, x))

    each(8, send_cot)

    finish_weights(0)
    drain(h1r, a2a_recv.at[0])
    depth_mask = line_mask(4)
    x = h1r[...].reshape(TOK, D).astype(F32)
    x = forward(x, w_t[0], wo_t[0], depth_mask, saves[0])
    pack8(x, h2s)
    gy_exchange(h2s, h2r, 1)

    spread(2)
    pass_runs(1)
    finish_weights(1)
    drain(h2r, a2a_recv.at[1])
    row_mask = line_mask(8)
    x = forward(unpack8(h2r), w_t[1], wo_t[1], row_mask, saves[1])
    pack4(x, h3s)

    def line_exchange(src, dst, n):
        def body(k):
            z, x = far(k)
            d = ((z + NZ - 1) % NZ) * NX + x
            send(src.at[d // 2, d % 2], dst.at[column // 2, column % 2], a2a_send.at[n], a2a_recv.at[n], (z, gy, x))

        each(NG - 1, body)
        pltpu.make_async_copy(
            src.at[line // 2, line % 2], dst.at[column // 2, column % 2], a2a_recv.at[n]
        ).start()

    def column_exchange(src, dst, n):
        def body(k):
            z, x = far(k)
            s = x * NZ + z
            send(src.at[s // 2, s % 2], dst.at[line // 2, line % 2], a2a_send.at[n], a2a_recv.at[n], (z, gy, x))

        each(NG - 1, body)
        pltpu.make_async_copy(
            src.at[column // 2, column % 2], dst.at[line // 2, line % 2], a2a_recv.at[n]
        ).start()

    line_exchange(h3s, h3r, 2)

    pass_runs(2)
    finish_weights(2)
    drain(cotr, cot_recv)
    g = dot(cotr[...].reshape(TOK, D), order[...], 1, 0).astype(BF16)
    drain(h3r, a2a_recv.at[2])
    forward(unpack4(h3r), w_t[2], None, None, saves[2])
    g = backward(g, w_t[2], wo_t[2], saves[2])
    pack4(g, g3s)
    column_exchange(g3s, g3r, 3)

    drain(g3r, a2a_recv.at[3])
    g = backward(unpack4(g3r).astype(BF16), w_t[1], wo_t[1], saves[1])
    pack8(g, g2s)
    gy_exchange(g2s, g2r, 4)

    drain(g2r, a2a_recv.at[4])
    g = backward(unpack8(g2r).astype(BF16), w_t[0], wo_t[0], saves[0])
    g1s[...] = dot(g.astype(BF16), order[...], 1, 1).astype(BF16).reshape(NZ, 32, D)
    gz_exchange(g1s, g1r, 5)

    drain(wparts.at[pl.ds(0, 7)], w_sems.at[0])
    drain(h1r.at[pl.ds(0, NZ - 1)], a2a_send.at[0])
    drain(cotr, cot_send)
    for layer in range(3):
        drain(ybuf.at[layer, pl.ds(0, 7)], y_send.at[layer])
        drain(gathered.at[layer, pl.ds(0, 12)], x_send.at[layer])
        drain(gathered.at[layer, pl.ds(0, 16)], c_send.at[layer])
    for n, ref in ((1, h2r), (4, g2r)):
        drain(ref.at[pl.ds(0, NY - 1)], a2a_send.at[n])
    for n, ref in ((2, h3r), (3, g3r)):
        drain(ref.at[pl.ds(0, 15)], a2a_send.at[n])
        drain(ref.at[15, pl.ds(0, 1)], a2a_send.at[n])
    drain(g1r.at[pl.ds(0, NZ - 1)], a2a_send.at[5])

    drain(g1r, a2a_recv.at[5])
    join_home(g1r, out)


def local(volume, cotangent, w_project, w_output):
    vmem = pltpu.VMEM
    save = [
        vmem((HEADS, TOK, TOK), BF16),
        vmem((TOK, 1), F32),
        vmem((TOK, D), BF16),
        vmem((2 * HEADS, 1, TOK), F32),
        vmem((3 * HEADS, HEAD, TOK), BF16),
    ]
    dma = pltpu.SemaphoreType.DMA
    scratch = [
        vmem((8, 16, D), BF16),
        vmem((3, ROWS, QKV), BF16),
        vmem((3, OUT, ROWS), BF16),
        *[vmem((NZ, 32, D), BF16)] * 2,
        *[vmem((NY, 32, 128), BF16)] * 2,
        *[vmem((16, 2, 16, 128), BF16)] * 4,
        *[vmem((NY, 32, 128), BF16)] * 2,
        *[vmem((NZ, 32, D), BF16)] * 2,
        vmem((NX, 16, D), BF16),
        vmem((D, D), BF16),
        vmem((8, CH, 128), BF16),
        vmem((3, 8, CH, 256), BF16),
        vmem((3, NG, CH, D), BF16),
        vmem((3, 3 * D, D), BF16),
        vmem((3, D, D), BF16),
        vmem((4 * D, D), F32),
        vmem((CH, 128), F32),
        *save * 3,
        dma((3,)),
        dma((6,)),
        dma((6,)),
        dma,
        dma,
        dma((2,)),
        dma((3,)),
        dma((3, 8)),
        dma((3,)),
        dma((16,)),
        dma((2, NZ)),
        dma((3,)),
        dma((3,)),
    ]
    block = volume.shape
    whole = pl.BlockSpec(memory_space=pltpu.VMEM)
    got = pl.pallas_call(
        kernel,
        out_shape=jax.ShapeDtypeStruct((8, 16, D), BF16),
        in_specs=[pl.BlockSpec(memory_space=pltpu.HBM)] * 4,
        out_specs=whole,
        scratch_shapes=scratch,
        compiler_params=pltpu.CompilerParams(
            collective_id=0, has_side_effects=True, vmem_limit_bytes=50_000_000
        ),
    )(
        *(
            pltpu.with_memory_space_constraint(array, pltpu.HBM)
            for array in (
                volume.reshape(8, 16, D),
                cotangent.reshape(8, 16, D),
                w_project,
                jnp.swapaxes(w_output, 1, 2),
            )
        )
    )
    return got.reshape(block)


def solution(mesh):
    return jax.shard_map(
        local,
        mesh=mesh,
        in_specs=(
            P("gz", "gy", "gx", None),
            P("gz", "gy", "gx", None),
            P(None, "gy", ("gz", "gx")),
            P(None, "gy", ("gz", "gx")),
        ),
        out_specs=P("gz", "gy", "gx", None),
        check_vma=False,
    )
```

```python
import functools

import jax
import jax.numpy as jnp
from jax import lax
from jax.experimental import pallas as pl
from jax.experimental.pallas import tpu as pltpu
from jax.sharding import PartitionSpec as P

MESH = pl.DeviceIdType.MESH
F32 = jnp.float32
BF16 = jnp.bfloat16
HEADS = 6
HEAD = 64
D = 384
EPS = 1e-06
TOK = 128
NZ, NY, NX = 4, 16, 8
NG = NZ * NX
QKV = 36
OUT = 12
CH = QKV + OUT
ROWS = 24


def ring(d, n):
    return min(d, n - d)


FAR_GY = sorted(
    ((dz, dy) for dz in range(8) for dy in range(2) if dz or dy), key=lambda p: -(ring(p[0], 8) + 4 * p[1])
)
FAR_GX = sorted(
    ((dx, m, dc) for dx in range(4) for m in range(4) for dc in range(2) if dx or m or dc),
    key=lambda p: -(ring(p[0], 4) + p[1]),
)


def dot(a, b, ca, cb):
    return lax.dot_general(a, b, (((ca,), (cb,)), ((), ())), preferred_element_type=F32)


def roll4(x):
    return pltpu.roll(x, 4, x.ndim - 2)


def low_half(shape):
    return lax.broadcasted_iota(jnp.int32, shape, len(shape) - 2) % 8 < 4


def swap_halves(u, v):
    low = low_half(u.shape)
    return jnp.where(low, u, roll4(v)), jnp.where(low, roll4(u), v)


def place(block):
    return (block % 2) * 8 + block // 2


def order_matrix():
    row = lax.broadcasted_iota(jnp.int32, (D, D), 0)
    col = lax.broadcasted_iota(jnp.int32, (D, D), 1)
    block = col // ROWS
    source = ((block % 8) * 2 + block // 8) * ROWS + col % ROWS
    return (row == source).astype(F32).astype(BF16)


def to_order(x):
    blocks = [x[ROWS * b : ROWS * (b + 1)] for b in range(NY)]
    return jnp.concatenate([blocks[(p % 8) * 2 + p // 8] for p in range(NY)], axis=0)


def from_order(x):
    blocks = [x[ROWS * p : ROWS * (p + 1)] for p in range(NY)]
    return jnp.concatenate([blocks[place(b)] for b in range(NY)], axis=0)


def forward(stream, w_t, wo_t, mask, save):
    inv = lax.rsqrt(jnp.mean(stream * stream, axis=-1, keepdims=True) + EPS)
    normed = (stream * inv).astype(BF16)
    packed = dot(w_t, normed, 1, 1)
    heads = packed.reshape(3, HEADS, HEAD, TOK)
    inv_qk = lax.rsqrt(jnp.mean(heads[:2] * heads[:2], axis=2, keepdims=True) + EPS)
    qk = (heads[:2] * inv_qk).astype(BF16)
    val = heads[2].astype(BF16)
    each_head = range(HEADS)
    scores = [dot(qk[1, h], qk[0, h], 0, 0) * (HEAD**-0.5) for h in each_head]
    powers = [jnp.exp(x) for x in scores]
    if mask is not None:
        powers = [jnp.where(mask, x, 0.0) for x in powers]
    attn = [(x / jnp.sum(x, axis=0, keepdims=True)).astype(BF16) for x in powers]
    mixed = jnp.concatenate([dot(val[h], attn[h], 1, 0) for h in each_head], axis=0)
    result = None
    if wo_t is not None:
        result = stream + dot(wo_t, to_order(mixed).astype(BF16), 1, 0).T
    for h in each_head:
        save["attn"][h] = attn[h]
    save["inv"][...] = inv
    save["normed"][...] = normed
    save["inv_qk"][...] = inv_qk.reshape(2 * HEADS, 1, TOK)
    save["qkv"][: 2 * HEADS] = qk.reshape(2 * HEADS, HEAD, TOK)
    save["qkv"][2 * HEADS :] = val
    return result


def grad_of_mixed(grad, wo_t):
    return from_order(dot(grad, wo_t, 1, 0).T).astype(BF16)


def backward(grad, w_t, mixed_grad, save):
    each_head = range(HEADS)
    q, k, v = ([save["qkv"][HEADS * i + h] for h in each_head] for i in range(3))
    attn = [save["attn"][h] for h in each_head]
    d_mixed = [mixed_grad[h * HEAD : (h + 1) * HEAD] for h in each_head]
    d_attn = [dot(v[h], d_mixed[h], 0, 0) for h in each_head]
    d_v = [dot(d_mixed[h], attn[h], 1, 1).astype(BF16) for h in each_head]
    d_scores = []
    for h in each_head:
        attn32 = attn[h].astype(F32)
        change = attn32 * (d_attn[h] - jnp.sum(d_attn[h] * attn32, axis=0, keepdims=True))
        d_scores.append((change * (HEAD**-0.5)).astype(BF16))
    d_q = [dot(k[h], d_scores[h], 1, 0) for h in each_head]
    d_k = [dot(q[h], d_scores[h], 1, 1) for h in each_head]
    packed_grad = []
    for at, (unit, d_unit) in enumerate(zip(q + k, d_q + d_k)):
        unit32 = unit.astype(F32)
        proj = jnp.mean(d_unit * unit32, axis=0, keepdims=True)
        packed_grad.append((save["inv_qk"][at] * (d_unit - unit32 * proj)).astype(BF16))
    packed_grad += d_v
    packed_grad = jnp.concatenate(packed_grad, axis=0)
    d_normed = dot(packed_grad, w_t, 0, 0)
    normed32 = save["normed"][...].astype(F32)
    proj = jnp.mean(d_normed * normed32, axis=-1, keepdims=True)
    return grad.astype(F32) + save["inv"][...] * (d_normed - normed32 * proj)


def line_mask(lines):
    row = lax.broadcasted_iota(jnp.int32, (TOK, TOK), 0)
    col = lax.broadcasted_iota(jnp.int32, (TOK, TOK), 1)
    return row % lines == col % lines


def split_home(block, out):
    x = block.astype(F32).reshape(4, 2, 2, 8, D)
    for half in range(2):
        low, high = swap_halves(x[:, 0, half], x[:, 1, half])
        out[2 * half] = low.reshape(32, D).astype(BF16)
        out[2 * half + 1] = high.reshape(32, D).astype(BF16)


def join_home(got, out):
    for half in range(2):
        u = got[2 * half].astype(F32).reshape(4, 8, D)
        v = got[2 * half + 1].astype(F32).reshape(4, 8, D)
        low, high = swap_halves(u, v)
        for m in range(4):
            out[2 * m, 8 * half : 8 * half + 8] = low[m].astype(BF16)
            out[2 * m + 1, 8 * half : 8 * half + 8] = high[m].astype(BF16)


def pack8(x, out):
    x = x.reshape(NY, 8, D)
    out[:, 0:16] = jnp.concatenate([x[:, :, 0:128], x[:, :, 128:256]], axis=1).astype(BF16)
    out[:, 16:32] = jnp.concatenate([x[:, :, 256:384], x[:, :, 256:384]], axis=1).astype(BF16)


def unpack8(got):
    x = got[...].astype(F32)
    return jnp.concatenate([x[:, 0:8], x[:, 8:16], x[:, 16:24]], axis=2).reshape(TOK, D)


def pack4(x, out):
    x = x.reshape(16, 8, D)
    first, second, third = x[:, :, 0:128], x[:, :, 128:256], x[:, :, 256:384]
    low, high = swap_halves(first, second)
    out[:, 0] = jnp.concatenate([low, third], axis=1).astype(BF16)
    out[:, 1] = jnp.concatenate([high, roll4(third)], axis=1).astype(BF16)


def unpack4(got):
    even, odd = got[:, 0].astype(F32), got[:, 1].astype(F32)
    first, second = swap_halves(even[:, 0:8], odd[:, 0:8])
    third = swap_halves(even[:, 8:16], odd[:, 8:16])[0]
    return jnp.concatenate([first, second, third], axis=2).reshape(TOK, D)


def own_chunk(w_ref, wo_ref, stage):
    rows = 3 * ROWS
    eye = (
        lax.broadcasted_iota(jnp.int32, (rows, 128), 0) == lax.broadcasted_iota(jnp.int32, (rows, 128), 1)
    ).astype(F32)
    block = jnp.concatenate([w_ref[i].astype(F32) for i in range(3)], axis=0).astype(BF16)
    stage[0:QKV] = dot(block, eye.astype(BF16), 0, 0)
    stage[QKV:CH] = sum(dot(wo_ref[i], eye[ROWS * i : ROWS * (i + 1)].astype(BF16), 1, 0) for i in range(3))
    return stage[...].astype(BF16)


def join_blocks(parts, pieces, tiles):
    lane = lax.broadcasted_iota(jnp.int32, (CH, 128), 1)
    joined = []
    for t in range(tiles):
        tile = None
        for n, (g, first) in enumerate(pieces):
            start = ROWS * n - 128 * t
            if start + ROWS <= 0 or start >= 128:
                continue
            piece = pltpu.roll(parts[g], (start - first) % 128, 1)
            tile = piece if tile is None else jnp.where(lane >= start, piece, tile)
        joined.append(tile)
    return joined


def half_roll(x):
    return pltpu.roll(x, 64, 1)


def join_halves(a, b):
    low = lax.broadcasted_iota(jnp.int32, (CH, 128), 1) < 64
    b0, b1 = half_roll(b[:, 0:128]), half_roll(b[:, 128:256])
    return jnp.concatenate([a[:, 0:128], jnp.where(low, a[:, 128:256], b0), jnp.where(low, b0, b1)], axis=1).astype(BF16)


def slot_of(unit):
    return (unit % 2) * 16 + (unit // 8) * 4 + (unit % 8) // 2


def compact(gathered, layer, w_t, wo_t, stage):
    for unit in range(NG):
        chunk = gathered[layer, slot_of(unit)].astype(F32)
        stage[QKV * unit : QKV * (unit + 1)] = chunk[:QKV]
        at = 3 * D + ROWS * place(unit // 2) + OUT * (unit % 2)
        stage[at : at + OUT] = chunk[QKV:]
    w_t[layer] = stage[: 3 * D].astype(BF16)
    wo_t[layer] = stage[3 * D :].astype(BF16)


def kernel(
    vol_hbm, cot_hbm, w_hbm, wo_hbm, out,
    vol, w_in, wo_in,
    h1s, h1r, h2s, h2r, h3s, h3r, g3s, g3r, g2s, g2r, g1s, g1r, cotr,
    order, wparts, ybuf, gathered, w_t, wo_t, wstage, cstage,
    *rest,
):
    saves = []
    for i in range(3):
        a, b, c, d, e = rest[5 * i : 5 * i + 5]
        saves.append(dict(attn=a, inv=b, normed=c, inv_qk=d, qkv=e))
    load_sems, a2a_send, a2a_recv, cot_send, cot_recv, w_sems, y_send, y_recv, x_send, x_first, x_recv, c_send, c_recv = rest[15:]
    gz, gy, gx = lax.axis_index("gz"), lax.axis_index("gy"), lax.axis_index("gx")
    core, ylo = gx % 2, gx // 2
    z, yhi = gy // 2, gy % 2
    y = yhi * 4 + ylo
    line = ((gz + NZ - 1) % NZ) * NX + gx
    column = gx * NZ + gz

    loads = [
        pltpu.make_async_copy(src, dst, load_sems.at[i])
        for i, (src, dst) in enumerate(((w_hbm, w_in), (wo_hbm, wo_in), (vol_hbm, vol)))
    ]
    for load in loads:
        load.start()

    def line_owner(d):
        return (d // NX + 1) % NZ, d % NX

    def column_owner(s):
        return s % NZ, s // NZ

    def send(src, dst, ssem, rsem, to):
        pltpu.make_async_remote_copy(
            src_ref=src, dst_ref=dst, send_sem=ssem, recv_sem=rsem, device_id=to, device_id_type=MESH
        ).start()

    def drain(ref, sem):
        pltpu.make_async_copy(ref, ref, sem).wait()

    def each(count, body):
        for k in range(count):
            body(k)

    def far(k):
        dx, m, dc = FAR_GX[k]
        to = (ylo, ylo + 1 - 2 * (ylo % 2), (ylo + 2) % 4, 3 - ylo)[m]
        return (gz + dx) % NZ, to * 2 + (core + dc) % 2

    barrier = pltpu.get_barrier_semaphore()

    def greet(to):
        pl.semaphore_signal(barrier, inc=1, device_id=to, device_id_type=MESH)

    def on_z(k):
        return gz, ((z + 1 + k) % 8) * 2 + yhi, gx

    def on_y(k):
        to = (y + 1 + k) % 8
        return gz, z * 2 + to // 4, (to % 4) * 2 + core

    def on_x(k):
        return (gz + 1 + k) % NZ, gy, gx

    sibling = (gz, gy, gx + 1 - 2 * core)
    each(7, lambda k: greet(on_z(k)))
    each(7, lambda k: greet(on_y(k)))
    each(3, lambda k: greet(on_x(k)))
    greet(sibling)

    loads[0].wait()
    loads[1].wait()
    wparts[z] = own_chunk(w_in, wo_in, cstage)
    pl.semaphore_wait(barrier, 18)

    each(7, lambda k: send(wparts.at[z], wparts.at[z], w_sems.at[0], w_sems.at[1], on_z(k)))

    def gz_exchange(src, dst, n):
        def body(k):
            to = (gz + 1 + k) % NZ
            send(src.at[to], dst.at[gz], a2a_send.at[n], a2a_recv.at[n], (to, gy, gx))

        each(NZ - 1, body)
        pltpu.make_async_copy(src.at[gz], dst.at[gz], a2a_recv.at[n]).start()

    def gy_exchange(src, dst, n):
        def body(k):
            dz, dy = FAR_GY[k]
            to = ((z + dz) % 8) * 2 + (yhi + dy) % 2
            send(src.at[to], dst.at[gy], a2a_send.at[n], a2a_recv.at[n], (gz, to, gx))

        each(NY - 1, body)
        pltpu.make_async_copy(src.at[gy], dst.at[gy], a2a_recv.at[n]).start()

    loads[2].wait()
    order[...] = order_matrix()
    split_home(dot(vol[...].reshape(TOK, D), order[...], 1, 0).reshape(8, 16, D), h1s)
    gz_exchange(h1s, h1r, 0)

    drain(wparts.at[pl.ds(0, 7)], w_sems.at[1])
    parts = wparts[...].astype(F32)

    def send_y(layer):
        tiles = join_blocks(parts, [(g, ROWS * layer) for g in range(8)], 2)
        ybuf[layer, y] = jnp.concatenate(tiles, axis=1).astype(BF16)
        block = ybuf.at[layer, y]
        each(7, lambda k: send(block, block, y_send.at[layer], y_recv.at[layer, y], on_y(k)))

    send_y(0)

    def run4(layer, at):
        return gathered.at[layer, pl.ds(core * 16 + at * 4, 4)]

    def send_x(layer, block, sem):
        each(3, lambda k: send(block, block, x_send.at[layer], sem, on_x(k)))

    def send_core(layer, block):
        send(block, block, c_send.at[layer], c_recv.at[layer], sibling)

    def join_y(layer, u):
        for half in range(2):
            at = half * 4 + u

            @pl.when(at != y)
            def _(at=at):
                drain(ybuf.at[layer, at], y_recv.at[layer, at])

        at = core * 16 + gz * 4 + u
        gathered[layer, at] = join_halves(ybuf[layer, u].astype(F32), ybuf[layer, 4 + u].astype(F32))
        return gathered.at[layer, at]

    def pass_y(k):
        u = (ylo + k) % 4
        block = join_y(0, u)
        for way in (1, 3):
            send(block, block, x_send.at[0], x_first.at[gz * 4 + u], ((gz + way) % NZ, gy, gx))
        send_core(0, block)

    for k in range(4):
        pass_y(k)
        if k == 1:
            send_y(1)

    def pass_x(way, k):
        at = ((gz + way) % NZ) * 4 + (ylo + k) % 4
        block = gathered.at[0, core * 16 + at]
        drain(block, x_first.at[at])
        if (way, k) in ((3, 0), (3, 1), (1, 2), (1, 3)):
            send(block, block, x_send.at[0], x_first.at[at], ((gz - way + NZ) % NZ, gy, gx))
        send_core(0, block)

    for k in range(4):
        pass_x(3, k)
        pass_x(1, k)
    def spread(layer):
        def body(k):
            join_y(layer, (ylo + k) % 4)

        each(4, body)
        block = run4(layer, gz)
        send_x(layer, block, x_recv.at[layer - 1, gz])
        send_core(layer, block)

    spread(1)
    send_y(2)
    for k in range(4):
        pass_x(2, k)

    def pass_runs(layer):
        def body(k):
            at = (gz + 1 + k) % NZ
            block = run4(layer, at)
            drain(block, x_recv.at[layer - 1, at])
            send_core(layer, block)

        each(3, body)

    def finish_weights(layer):
        drain(gathered.at[layer, pl.ds(0, 16)], c_recv.at[layer])
        compact(gathered, layer, w_t, wo_t, wstage)


    def send_cot(k):
        z, x = line_owner(2 * gy + k % 2)
        send(cot_hbm.at[k], cotr.at[gx], cot_send, cot_recv, (z, 4 * gz + k // 2, x))

    each(8, send_cot)

    finish_weights(0)
    drain(h1r, a2a_recv.at[0])
    depth_mask = line_mask(4)
    x = h1r[...].reshape(TOK, D).astype(F32)
    x = forward(x, w_t[0], wo_t[0], depth_mask, saves[0])
    pack8(x, h2s)
    gy_exchange(h2s, h2r, 1)

    spread(2)
    pass_runs(1)
    finish_weights(1)
    drain(h2r, a2a_recv.at[1])
    row_mask = line_mask(8)
    x = forward(unpack8(h2r), w_t[1], wo_t[1], row_mask, saves[1])
    pack4(x, h3s)

    def line_exchange(src, dst, n):
        def body(k):
            z, x = far(k)
            d = ((z + NZ - 1) % NZ) * NX + x
            send(src.at[d // 2, d % 2], dst.at[column // 2, column % 2], a2a_send.at[n], a2a_recv.at[n], (z, gy, x))

        each(NG - 1, body)
        pltpu.make_async_copy(
            src.at[line // 2, line % 2], dst.at[column // 2, column % 2], a2a_recv.at[n]
        ).start()

    def column_exchange(src, dst, n):
        def body(k):
            z, x = far(k)
            s = x * NZ + z
            send(src.at[s // 2, s % 2], dst.at[line // 2, line % 2], a2a_send.at[n], a2a_recv.at[n], (z, gy, x))

        each(NG - 1, body)
        pltpu.make_async_copy(
            src.at[column // 2, column % 2], dst.at[line // 2, line % 2], a2a_recv.at[n]
        ).start()

    line_exchange(h3s, h3r, 2)

    pass_runs(2)
    finish_weights(2)
    drain(cotr, cot_recv)
    g = dot(cotr[...].reshape(TOK, D), order[...], 1, 0).astype(BF16)
    mixed_grad = grad_of_mixed(g, wo_t[2])
    drain(h3r, a2a_recv.at[2])
    forward(unpack4(h3r), w_t[2], None, None, saves[2])
    g = backward(g, w_t[2], mixed_grad, saves[2])
    pack4(g, g3s)
    column_exchange(g3s, g3r, 3)

    drain(g3r, a2a_recv.at[3])
    g = unpack4(g3r).astype(BF16)
    g = backward(g, w_t[1], grad_of_mixed(g, wo_t[1]), saves[1])
    pack8(g, g2s)
    gy_exchange(g2s, g2r, 4)

    drain(wparts.at[pl.ds(0, 7)], w_sems.at[0])
    drain(h1r.at[pl.ds(0, NZ - 1)], a2a_send.at[0])
    drain(cotr, cot_send)
    for layer in range(3):
        drain(ybuf.at[layer, pl.ds(0, 7)], y_send.at[layer])
        drain(gathered.at[layer, pl.ds(0, 12)], x_send.at[layer])
        drain(gathered.at[layer, pl.ds(0, 16)], c_send.at[layer])
    for n, ref in ((1, h2r), (4, g2r)):
        drain(ref.at[pl.ds(0, NY - 1)], a2a_send.at[n])
    for n, ref in ((2, h3r), (3, g3r)):
        drain(ref.at[pl.ds(0, 15)], a2a_send.at[n])
        drain(ref.at[15, pl.ds(0, 1)], a2a_send.at[n])
    drain(g2r, a2a_recv.at[4])
    g = unpack8(g2r).astype(BF16)
    g = backward(g, w_t[0], grad_of_mixed(g, wo_t[0]), saves[0])
    g1s[...] = dot(g.astype(BF16), order[...], 1, 1).astype(BF16).reshape(NZ, 32, D)
    gz_exchange(g1s, g1r, 5)

    drain(g1r.at[pl.ds(0, NZ - 1)], a2a_send.at[5])
    drain(g1r, a2a_recv.at[5])
    join_home(g1r, out)


def local(volume, cotangent, w_project, w_output):
    vmem = pltpu.VMEM
    save = [
        vmem((HEADS, TOK, TOK), BF16),
        vmem((TOK, 1), F32),
        vmem((TOK, D), BF16),
        vmem((2 * HEADS, 1, TOK), F32),
        vmem((3 * HEADS, HEAD, TOK), BF16),
    ]
    dma = pltpu.SemaphoreType.DMA
    scratch = [
        vmem((8, 16, D), BF16),
        vmem((3, ROWS, QKV), BF16),
        vmem((3, OUT, ROWS), BF16),
        *[vmem((NZ, 32, D), BF16)] * 2,
        *[vmem((NY, 32, 128), BF16)] * 2,
        *[vmem((16, 2, 16, 128), BF16)] * 4,
        *[vmem((NY, 32, 128), BF16)] * 2,
        *[vmem((NZ, 32, D), BF16)] * 2,
        vmem((NX, 16, D), BF16),
        vmem((D, D), BF16),
        vmem((8, CH, 128), BF16),
        vmem((3, 8, CH, 256), BF16),
        vmem((3, NG, CH, D), BF16),
        vmem((3, 3 * D, D), BF16),
        vmem((3, D, D), BF16),
        vmem((4 * D, D), F32),
        vmem((CH, 128), F32),
        *save * 3,
        dma((3,)),
        dma((6,)),
        dma((6,)),
        dma,
        dma,
        dma((2,)),
        dma((3,)),
        dma((3, 8)),
        dma((3,)),
        dma((16,)),
        dma((2, NZ)),
        dma((3,)),
        dma((3,)),
    ]
    block = volume.shape
    whole = pl.BlockSpec(memory_space=pltpu.VMEM)
    got = pl.pallas_call(
        kernel,
        out_shape=jax.ShapeDtypeStruct((8, 16, D), BF16),
        in_specs=[pl.BlockSpec(memory_space=pltpu.HBM)] * 4,
        out_specs=whole,
        scratch_shapes=scratch,
        compiler_params=pltpu.CompilerParams(
            collective_id=0, has_side_effects=True, vmem_limit_bytes=50_000_000
        ),
    )(
        *(
            pltpu.with_memory_space_constraint(array, pltpu.HBM)
            for array in (
                volume.reshape(8, 16, D),
                cotangent.reshape(8, 16, D),
                w_project,
                jnp.swapaxes(w_output, 1, 2),
            )
        )
    )
    return got.reshape(block)


def solution(mesh):
    return jax.shard_map(
        local,
        mesh=mesh,
        in_specs=(
            P("gz", "gy", "gx", None),
            P("gz", "gy", "gx", None),
            P(None, "gy", ("gz", "gx")),
            P(None, "gy", ("gz", "gx")),
        ),
        out_specs=P("gz", "gy", "gx", None),
        check_vma=False,
    )
```

```python
import functools

import jax
import jax.numpy as jnp
from jax import lax
from jax.experimental import pallas as pl
from jax.experimental.pallas import tpu as pltpu
from jax.sharding import PartitionSpec as P

MESH = pl.DeviceIdType.MESH
F32 = jnp.float32
BF16 = jnp.bfloat16
HEADS = 6
HEAD = 64
D = 384
EPS = 1e-06
TOK = 128
NZ, NY, NX = 4, 16, 8
NG = NZ * NX
QKV = 36
OUT = 12
CH = QKV + OUT
ROWS = 24


def ring(d, n):
    return min(d, n - d)


FAR_GY = sorted(
    ((dz, dy) for dz in range(8) for dy in range(2) if dz or dy), key=lambda p: -(ring(p[0], 8) + 4 * p[1])
)
FAR_GX = sorted(
    ((dx, m, dc) for dx in range(4) for m in range(4) for dc in range(2) if dx or m or dc),
    key=lambda p: -(ring(p[0], 4) + p[1]),
)


def dot(a, b, ca, cb):
    return lax.dot_general(a, b, (((ca,), (cb,)), ((), ())), preferred_element_type=F32)


def roll4(x):
    return pltpu.roll(x, 4, x.ndim - 2)


def low_half(shape):
    return lax.broadcasted_iota(jnp.int32, shape, len(shape) - 2) % 8 < 4


def swap_halves(u, v):
    low = low_half(u.shape)
    return jnp.where(low, u, roll4(v)), jnp.where(low, roll4(u), v)


def place(block):
    return (block % 2) * 8 + block // 2


def order_matrix():
    row = lax.broadcasted_iota(jnp.int32, (D, D), 0)
    col = lax.broadcasted_iota(jnp.int32, (D, D), 1)
    block = col // ROWS
    source = ((block % 8) * 2 + block // 8) * ROWS + col % ROWS
    return (row == source).astype(F32).astype(BF16)


def to_order(x):
    blocks = [x[ROWS * b : ROWS * (b + 1)] for b in range(NY)]
    return jnp.concatenate([blocks[(p % 8) * 2 + p // 8] for p in range(NY)], axis=0)


def from_order(x):
    blocks = [x[ROWS * p : ROWS * (p + 1)] for p in range(NY)]
    return jnp.concatenate([blocks[place(b)] for b in range(NY)], axis=0)


def forward(stream, w_t, wo_t, mask, save):
    inv = lax.rsqrt(jnp.mean(stream * stream, axis=-1, keepdims=True) + EPS)
    normed = (stream * inv).astype(BF16)
    packed = dot(w_t, normed, 1, 1)
    heads = packed.reshape(3, HEADS, HEAD, TOK)
    inv_qk = lax.rsqrt(jnp.mean(heads[:2] * heads[:2], axis=2, keepdims=True) + EPS)
    qk = (heads[:2] * inv_qk).astype(BF16)
    val = heads[2].astype(BF16)
    each_head = range(HEADS)
    scores = [dot(qk[1, h], qk[0, h], 0, 0) * (HEAD**-0.5) for h in each_head]
    powers = [jnp.exp(x) for x in scores]
    if mask is not None:
        powers = [jnp.where(mask, x, 0.0) for x in powers]
    attn = [(x / jnp.sum(x, axis=0, keepdims=True)).astype(BF16) for x in powers]
    mixed = jnp.concatenate([dot(val[h], attn[h], 1, 0) for h in each_head], axis=0)
    result = None
    if wo_t is not None:
        result = stream + dot(wo_t, to_order(mixed).astype(BF16), 1, 0).T
    for h in each_head:
        save["attn"][h] = attn[h]
    save["inv"][...] = inv
    save["normed"][...] = normed
    save["inv_qk"][...] = inv_qk.reshape(2 * HEADS, 1, TOK)
    save["qkv"][: 2 * HEADS] = qk.reshape(2 * HEADS, HEAD, TOK)
    save["qkv"][2 * HEADS :] = val
    return result


def grad_of_mixed(grad, wo_t):
    return from_order(dot(grad, wo_t, 1, 0).T).astype(BF16)


def backward(grad, w_t, mixed_grad, save):
    each_head = range(HEADS)
    q, k, v = ([save["qkv"][HEADS * i + h] for h in each_head] for i in range(3))
    attn = [save["attn"][h] for h in each_head]
    d_mixed = [mixed_grad[h * HEAD : (h + 1) * HEAD] for h in each_head]
    d_attn = [dot(v[h], d_mixed[h], 0, 0) for h in each_head]
    d_v = [dot(d_mixed[h], attn[h], 1, 1).astype(BF16) for h in each_head]
    d_scores = []
    for h in each_head:
        attn32 = attn[h].astype(F32)
        change = attn32 * (d_attn[h] - jnp.sum(d_attn[h] * attn32, axis=0, keepdims=True))
        d_scores.append((change * (HEAD**-0.5)).astype(BF16))
    d_q = [dot(k[h], d_scores[h], 1, 0) for h in each_head]
    d_k = [dot(q[h], d_scores[h], 1, 1) for h in each_head]
    packed_grad = []
    for at, (unit, d_unit) in enumerate(zip(q + k, d_q + d_k)):
        unit32 = unit.astype(F32)
        proj = jnp.mean(d_unit * unit32, axis=0, keepdims=True)
        packed_grad.append((save["inv_qk"][at] * (d_unit - unit32 * proj)).astype(BF16))
    packed_grad += d_v
    packed_grad = jnp.concatenate(packed_grad, axis=0)
    d_normed = dot(packed_grad, w_t, 0, 0)
    normed32 = save["normed"][...].astype(F32)
    proj = jnp.mean(d_normed * normed32, axis=-1, keepdims=True)
    return grad.astype(F32) + save["inv"][...] * (d_normed - normed32 * proj)


def line_mask(lines):
    row = lax.broadcasted_iota(jnp.int32, (TOK, TOK), 0)
    col = lax.broadcasted_iota(jnp.int32, (TOK, TOK), 1)
    return row % lines == col % lines


def split_home(block, out):
    x = block.astype(F32).reshape(4, 2, 2, 8, D)
    for half in range(2):
        low, high = swap_halves(x[:, 0, half], x[:, 1, half])
        out[2 * half] = low.reshape(32, D).astype(BF16)
        out[2 * half + 1] = high.reshape(32, D).astype(BF16)


def join_home(got, out):
    for half in range(2):
        u = got[2 * half].astype(F32).reshape(4, 8, D)
        v = got[2 * half + 1].astype(F32).reshape(4, 8, D)
        low, high = swap_halves(u, v)
        for m in range(4):
            out[2 * m, 8 * half : 8 * half + 8] = low[m].astype(BF16)
            out[2 * m + 1, 8 * half : 8 * half + 8] = high[m].astype(BF16)


def pack8(x, out):
    x = x.reshape(NY, 8, D)
    out[:, 0:16] = jnp.concatenate([x[:, :, 0:128], x[:, :, 128:256]], axis=1).astype(BF16)
    out[:, 16:32] = jnp.concatenate([x[:, :, 256:384], x[:, :, 256:384]], axis=1).astype(BF16)


def unpack8(got):
    x = got[...].astype(F32)
    return jnp.concatenate([x[:, 0:8], x[:, 8:16], x[:, 16:24]], axis=2).reshape(TOK, D)


def pack4(x, out):
    x = x.reshape(16, 8, D)
    first, second, third = x[:, :, 0:128], x[:, :, 128:256], x[:, :, 256:384]
    low, high = swap_halves(first, second)
    out[:, 0] = jnp.concatenate([low, third], axis=1).astype(BF16)
    out[:, 1] = jnp.concatenate([high, roll4(third)], axis=1).astype(BF16)


def unpack4(got):
    even, odd = got[:, 0].astype(F32), got[:, 1].astype(F32)
    first, second = swap_halves(even[:, 0:8], odd[:, 0:8])
    third = swap_halves(even[:, 8:16], odd[:, 8:16])[0]
    return jnp.concatenate([first, second, third], axis=2).reshape(TOK, D)


def own_chunk(w_ref, wo_ref, stage):
    rows = 3 * ROWS
    eye = (
        lax.broadcasted_iota(jnp.int32, (rows, 128), 0) == lax.broadcasted_iota(jnp.int32, (rows, 128), 1)
    ).astype(F32)
    block = jnp.concatenate([w_ref[i].astype(F32) for i in range(3)], axis=0).astype(BF16)
    stage[0:QKV] = dot(block, eye.astype(BF16), 0, 0)
    stage[QKV:CH] = sum(dot(wo_ref[i], eye[ROWS * i : ROWS * (i + 1)].astype(BF16), 1, 0) for i in range(3))
    return stage[...].astype(BF16)


def join_blocks(parts, pieces, tiles):
    lane = lax.broadcasted_iota(jnp.int32, (CH, 128), 1)
    joined = []
    for t in range(tiles):
        tile = None
        for n, (g, first) in enumerate(pieces):
            start = ROWS * n - 128 * t
            if start + ROWS <= 0 or start >= 128:
                continue
            piece = pltpu.roll(parts[g], (start - first) % 128, 1)
            tile = piece if tile is None else jnp.where(lane >= start, piece, tile)
        joined.append(tile)
    return joined


def half_roll(x):
    return pltpu.roll(x, 64, 1)


def join_halves(a, b):
    low = lax.broadcasted_iota(jnp.int32, (CH, 128), 1) < 64
    b0, b1 = half_roll(b[:, 0:128]), half_roll(b[:, 128:256])
    return jnp.concatenate([a[:, 0:128], jnp.where(low, a[:, 128:256], b0), jnp.where(low, b0, b1)], axis=1).astype(BF16)


def slot_of(unit):
    return (unit % 2) * 16 + (unit // 8) * 4 + (unit % 8) // 2


def compact(gathered, layer, w_t, wo_t, stage):
    for unit in range(NG):
        chunk = gathered[layer, slot_of(unit)].astype(F32)
        stage[QKV * unit : QKV * (unit + 1)] = chunk[:QKV]
        at = 3 * D + ROWS * place(unit // 2) + OUT * (unit % 2)
        stage[at : at + OUT] = chunk[QKV:]
    w_t[layer] = stage[: 3 * D].astype(BF16)
    wo_t[layer] = stage[3 * D :].astype(BF16)


def kernel(
    vol_hbm, cot_hbm, w_hbm, wo_hbm, out,
    vol, w_in, wo_in,
    h1s, h1r, h2s, h2r, h3s, h3r, g3s, g3r, g2s, g2r, g1s, g1r, cotr,
    order, wparts, ybuf, gathered, w_t, wo_t, wstage, cstage,
    *rest,
):
    saves = []
    for i in range(3):
        a, b, c, d, e = rest[5 * i : 5 * i + 5]
        saves.append(dict(attn=a, inv=b, normed=c, inv_qk=d, qkv=e))
    load_sems, a2a_send, a2a_recv, cot_send, cot_recv, w_sems, y_send, y_recv, x_send, x_first, x_recv, c_send, c_recv = rest[15:]
    gz, gy, gx = lax.axis_index("gz"), lax.axis_index("gy"), lax.axis_index("gx")
    core, ylo = gx % 2, gx // 2
    z, yhi = gy // 2, gy % 2
    y = yhi * 4 + ylo
    line = ((gz + NZ - 1) % NZ) * NX + gx
    column = gx * NZ + gz

    loads = [
        pltpu.make_async_copy(src, dst, load_sems.at[i])
        for i, (src, dst) in enumerate(((w_hbm, w_in), (wo_hbm, wo_in), (vol_hbm, vol)))
    ]
    for load in loads:
        load.start()

    def line_owner(d):
        return (d // NX + 1) % NZ, d % NX

    def column_owner(s):
        return s % NZ, s // NZ

    def send(src, dst, ssem, rsem, to):
        pltpu.make_async_remote_copy(
            src_ref=src, dst_ref=dst, send_sem=ssem, recv_sem=rsem, device_id=to, device_id_type=MESH
        ).start()

    def drain(ref, sem):
        pltpu.make_async_copy(ref, ref, sem).wait()

    def each(count, body):
        for k in range(count):
            body(k)

    def far(k):
        dx, m, dc = FAR_GX[k]
        to = (ylo, ylo + 1 - 2 * (ylo % 2), (ylo + 2) % 4, 3 - ylo)[m]
        return (gz + dx) % NZ, to * 2 + (core + dc) % 2

    barrier = pltpu.get_barrier_semaphore()

    def greet(to):
        pl.semaphore_signal(barrier, inc=1, device_id=to, device_id_type=MESH)

    def on_z(k):
        return gz, ((z + 1 + k) % 8) * 2 + yhi, gx

    def on_y(k):
        to = (y + 1 + k) % 8
        return gz, z * 2 + to // 4, (to % 4) * 2 + core

    def on_x(k):
        return (gz + 1 + k) % NZ, gy, gx

    sibling = (gz, gy, gx + 1 - 2 * core)
    each(7, lambda k: greet(on_z(k)))
    each(7, lambda k: greet(on_y(k)))
    each(3, lambda k: greet(on_x(k)))
    greet(sibling)

    loads[0].wait()
    loads[1].wait()
    wparts[z] = own_chunk(w_in, wo_in, cstage)
    pl.semaphore_wait(barrier, 18)

    each(7, lambda k: send(wparts.at[z], wparts.at[z], w_sems.at[0], w_sems.at[1], on_z(k)))

    def gz_exchange(src, dst, n):
        def body(k):
            to = (gz + 1 + k) % NZ
            send(src.at[to], dst.at[gz], a2a_send.at[n], a2a_recv.at[n], (to, gy, gx))

        each(NZ - 1, body)
        pltpu.make_async_copy(src.at[gz], dst.at[gz], a2a_recv.at[n]).start()

    def gy_exchange(src, dst, n):
        def body(k):
            dz, dy = FAR_GY[k]
            to = ((z + dz) % 8) * 2 + (yhi + dy) % 2
            send(src.at[to], dst.at[gy], a2a_send.at[n], a2a_recv.at[n], (gz, to, gx))

        each(NY - 1, body)
        pltpu.make_async_copy(src.at[gy], dst.at[gy], a2a_recv.at[n]).start()

    loads[2].wait()
    order[...] = order_matrix()
    split_home(dot(vol[...].reshape(TOK, D), order[...], 1, 0).reshape(8, 16, D), h1s)
    gz_exchange(h1s, h1r, 0)

    drain(wparts.at[pl.ds(0, 7)], w_sems.at[1])
    parts = wparts[...].astype(F32)

    def send_y(layer):
        tiles = join_blocks(parts, [(g, ROWS * layer) for g in range(8)], 2)
        ybuf[layer, y] = jnp.concatenate(tiles, axis=1).astype(BF16)
        block = ybuf.at[layer, y]
        each(7, lambda k: send(block, block, y_send.at[layer], y_recv.at[layer, y], on_y(k)))

    send_y(0)

    def run4(layer, at):
        return gathered.at[layer, pl.ds(core * 16 + at * 4, 4)]

    def send_x(layer, block, sem):
        each(3, lambda k: send(block, block, x_send.at[layer], sem, on_x(k)))

    def send_core(layer, block):
        send(block, block, c_send.at[layer], c_recv.at[layer], sibling)

    def join_y(layer, u):
        for half in range(2):
            at = half * 4 + u

            @pl.when(at != y)
            def _(at=at):
                drain(ybuf.at[layer, at], y_recv.at[layer, at])

        at = core * 16 + gz * 4 + u
        gathered[layer, at] = join_halves(ybuf[layer, u].astype(F32), ybuf[layer, 4 + u].astype(F32))
        return gathered.at[layer, at]

    def pass_y(k):
        u = (ylo + k) % 4
        block = join_y(0, u)
        for way in (1, 3):
            send(block, block, x_send.at[0], x_first.at[gz * 4 + u], ((gz + way) % NZ, gy, gx))
        send_core(0, block)

    for k in range(4):
        pass_y(k)
        if k == 1:
            send_y(1)

    def pass_x(way, k):
        at = ((gz + way) % NZ) * 4 + (ylo + k) % 4
        block = gathered.at[0, core * 16 + at]
        drain(block, x_first.at[at])
        if (way, k) in ((3, 0), (3, 1), (1, 2), (1, 3)):
            send(block, block, x_send.at[0], x_first.at[at], ((gz - way + NZ) % NZ, gy, gx))
        send_core(0, block)

    for k in range(4):
        pass_x(3, k)
        pass_x(1, k)
    def spread(layer):
        def body(k):
            join_y(layer, (ylo + k) % 4)

        each(4, body)
        block = run4(layer, gz)
        send_x(layer, block, x_recv.at[layer - 1, gz])
        send_core(layer, block)

    spread(1)
    send_y(2)
    for k in range(4):
        pass_x(2, k)

    def pass_runs(layer):
        def body(k):
            at = (gz + 1 + k) % NZ
            block = run4(layer, at)
            drain(block, x_recv.at[layer - 1, at])
            send_core(layer, block)

        each(3, body)

    def finish_weights(layer):
        drain(gathered.at[layer, pl.ds(0, 16)], c_recv.at[layer])
        compact(gathered, layer, w_t, wo_t, wstage)


    finish_weights(0)
    drain(h1r, a2a_recv.at[0])
    depth_mask = line_mask(4)
    x = h1r[...].reshape(TOK, D).astype(F32)
    x = forward(x, w_t[0], wo_t[0], depth_mask, saves[0])
    pack8(x, h2s)
    gy_exchange(h2s, h2r, 1)

    spread(2)
    pass_runs(1)
    finish_weights(1)
    def send_cot(k):
        z, x = line_owner(2 * gy + k % 2)
        send(cot_hbm.at[k], cotr.at[gx], cot_send, cot_recv, (z, 4 * gz + k // 2, x))

    each(8, send_cot)

    drain(h2r, a2a_recv.at[1])
    row_mask = line_mask(8)
    x = forward(unpack8(h2r), w_t[1], wo_t[1], row_mask, saves[1])
    pack4(x, h3s)

    def line_exchange(src, dst, n):
        def body(k):
            z, x = far(k)
            d = ((z + NZ - 1) % NZ) * NX + x
            send(src.at[d // 2, d % 2], dst.at[column // 2, column % 2], a2a_send.at[n], a2a_recv.at[n], (z, gy, x))

        each(NG - 1, body)
        pltpu.make_async_copy(
            src.at[line // 2, line % 2], dst.at[column // 2, column % 2], a2a_recv.at[n]
        ).start()

    def column_exchange(src, dst, n):
        def body(k):
            z, x = far(k)
            s = x * NZ + z
            send(src.at[s // 2, s % 2], dst.at[line // 2, line % 2], a2a_send.at[n], a2a_recv.at[n], (z, gy, x))

        each(NG - 1, body)
        pltpu.make_async_copy(
            src.at[column // 2, column % 2], dst.at[line // 2, line % 2], a2a_recv.at[n]
        ).start()

    line_exchange(h3s, h3r, 2)

    pass_runs(2)
    finish_weights(2)
    drain(cotr, cot_recv)
    g = dot(cotr[...].reshape(TOK, D), order[...], 1, 0).astype(BF16)
    mixed_grad = grad_of_mixed(g, wo_t[2])
    drain(h3r, a2a_recv.at[2])
    forward(unpack4(h3r), w_t[2], None, None, saves[2])
    g = backward(g, w_t[2], mixed_grad, saves[2])
    pack4(g, g3s)
    column_exchange(g3s, g3r, 3)

    drain(g3r, a2a_recv.at[3])
    g = unpack4(g3r).astype(BF16)
    g = backward(g, w_t[1], grad_of_mixed(g, wo_t[1]), saves[1])
    pack8(g, g2s)
    gy_exchange(g2s, g2r, 4)

    drain(wparts.at[pl.ds(0, 7)], w_sems.at[0])
    drain(h1r.at[pl.ds(0, NZ - 1)], a2a_send.at[0])
    drain(cotr, cot_send)
    for layer in range(3):
        drain(ybuf.at[layer, pl.ds(0, 7)], y_send.at[layer])
        drain(gathered.at[layer, pl.ds(0, 12)], x_send.at[layer])
        drain(gathered.at[layer, pl.ds(0, 16)], c_send.at[layer])
    for n, ref in ((1, h2r), (4, g2r)):
        drain(ref.at[pl.ds(0, NY - 1)], a2a_send.at[n])
    for n, ref in ((2, h3r), (3, g3r)):
        drain(ref.at[pl.ds(0, 15)], a2a_send.at[n])
        drain(ref.at[15, pl.ds(0, 1)], a2a_send.at[n])
    drain(g2r, a2a_recv.at[4])
    g = unpack8(g2r).astype(BF16)
    g = backward(g, w_t[0], grad_of_mixed(g, wo_t[0]), saves[0])
    g1s[...] = dot(g.astype(BF16), order[...], 1, 1).astype(BF16).reshape(NZ, 32, D)
    gz_exchange(g1s, g1r, 5)

    drain(g1r.at[pl.ds(0, NZ - 1)], a2a_send.at[5])
    drain(g1r, a2a_recv.at[5])
    join_home(g1r, out)


def local(volume, cotangent, w_project, w_output):
    vmem = pltpu.VMEM
    save = [
        vmem((HEADS, TOK, TOK), BF16),
        vmem((TOK, 1), F32),
        vmem((TOK, D), BF16),
        vmem((2 * HEADS, 1, TOK), F32),
        vmem((3 * HEADS, HEAD, TOK), BF16),
    ]
    dma = pltpu.SemaphoreType.DMA
    scratch = [
        vmem((8, 16, D), BF16),
        vmem((3, ROWS, QKV), BF16),
        vmem((3, OUT, ROWS), BF16),
        *[vmem((NZ, 32, D), BF16)] * 2,
        *[vmem((NY, 32, 128), BF16)] * 2,
        *[vmem((16, 2, 16, 128), BF16)] * 4,
        *[vmem((NY, 32, 128), BF16)] * 2,
        *[vmem((NZ, 32, D), BF16)] * 2,
        vmem((NX, 16, D), BF16),
        vmem((D, D), BF16),
        vmem((8, CH, 128), BF16),
        vmem((3, 8, CH, 256), BF16),
        vmem((3, NG, CH, D), BF16),
        vmem((3, 3 * D, D), BF16),
        vmem((3, D, D), BF16),
        vmem((4 * D, D), F32),
        vmem((CH, 128), F32),
        *save * 3,
        dma((3,)),
        dma((6,)),
        dma((6,)),
        dma,
        dma,
        dma((2,)),
        dma((3,)),
        dma((3, 8)),
        dma((3,)),
        dma((16,)),
        dma((2, NZ)),
        dma((3,)),
        dma((3,)),
    ]
    block = volume.shape
    whole = pl.BlockSpec(memory_space=pltpu.VMEM)
    got = pl.pallas_call(
        kernel,
        out_shape=jax.ShapeDtypeStruct((8, 16, D), BF16),
        in_specs=[pl.BlockSpec(memory_space=pltpu.HBM)] * 4,
        out_specs=whole,
        scratch_shapes=scratch,
        compiler_params=pltpu.CompilerParams(
            collective_id=0, has_side_effects=True, vmem_limit_bytes=50_000_000
        ),
    )(
        *(
            pltpu.with_memory_space_constraint(array, pltpu.HBM)
            for array in (
                volume.reshape(8, 16, D),
                cotangent.reshape(8, 16, D),
                w_project,
                jnp.swapaxes(w_output, 1, 2),
            )
        )
    )
    return got.reshape(block)


def solution(mesh):
    return jax.shard_map(
        local,
        mesh=mesh,
        in_specs=(
            P("gz", "gy", "gx", None),
            P("gz", "gy", "gx", None),
            P(None, "gy", ("gz", "gx")),
            P(None, "gy", ("gz", "gx")),
        ),
        out_specs=P("gz", "gy", "gx", None),
        check_vma=False,
    )
```
